1024 devices in a mesh: group: 16 (over y, core), outer: 64 (over z, x).
Axes of the slice: x: 8, y: 8, z: 8, core: 2. Of those that a mesh axis runs over, the one named last changes fastest.
Arguments:
- features: bfloat16 [262144, 1024], P(('group', 'outer')), may hold values from -6 to 6
- basis_weights: bfloat16 [2, 1024, 512], replicated, may hold values from -0.1875 to 0.1875
- self_weight: bfloat16 [1024, 512], replicated, may hold values from -0.1875 to 0.1875
- coefficients: float32 [3, 2], replicated, may hold values from -4 to 4
- counts: int32 [2048, 3, 4, 128, 128], P(('group', 'outer')), may hold values from 0 to 3, as said below
- tile_source: int32 [2048, 3, 4], P(('group', 'outer')), may hold values from 0 to 5, as said below
- send_rows: int32 [16384, 16], P(('group', 'outer')), may hold values from 0 to 255
- edge_rows: int32 [2048, 128], P(('group', 'outer')), may hold values from 0 to 255
- cotangent: bfloat16 [262144, 512], P(('group', 'outer')), may hold values from -24 to 24
Outputs:
- layer_out: bfloat16 [262144, 512], P(('group', 'outer'))
- basis_grad: float32 [2, 1024, 512], P(None, 'group', 'outer')
The draws below stay inside these ranges and needn't reach their ends.
Inputs may be any that keep to these rules, and one draw needn't show every extreme that they name: `counts`: for each destination block and relation the tiles that hold an edge come first: after the first all-zero tile every later tile of that block and relation is zero. The first tile always holds an edge, and some destination block and relation has all 4 tiles holding edges. `tile_source`: on each partition the first tiles of its 6 destination blocks and relations name all 6 source blocks.
All inputs are finite; a program needn't handle non-finite values.
Results may differ from the reference program's by a relative error of at most 0.0048.
Values may be sent and summed in bfloat16 or wider, within the bound.
A program may use at most 32 MiB of HBM per device.

```python
import math
import jax
import jax.numpy as jnp
from jax import lax

H_IN = 1024
OUT = 512
R = 3
B = 2
BLOCK = 128
NBLK = 2
K = 4
HALO = 128
NODES = 262144
DBLK = 2048
PEER_ROWS = 16
SRC = 6
N_GROUP = 16
N_OUTER = 64
DEVICES = 1024


def tile_plan(key):
    subkeys = jax.random.split(key, 4)
    first_draw = jax.random.randint(subkeys[0], (DBLK, R), 0, 4)
    second_draw = jax.random.randint(subkeys[1], (DBLK, R), 0, 4)
    live_tiles = jnp.minimum(1 + first_draw * second_draw // 3, K)
    forced_pair = jax.random.randint(subkeys[2], (), 0, DBLK * R)
    flat_index = jnp.arange(DBLK * R, dtype=jnp.int32).reshape(DBLK, R)
    live_tiles = jnp.where(flat_index == forced_pair, K, live_tiles)
    partitions = DBLK // NBLK
    scores = jax.random.randint(subkeys[3], (partitions, SRC), 0, 1 << 20) * SRC + jnp.arange(SRC, dtype=jnp.int32)
    ordering = jnp.argsort(scores, axis=1).astype(jnp.int32)
    pair_slot = jnp.arange(NBLK * R, dtype=jnp.int32) % SRC
    first_source = ordering[:, pair_slot].reshape(DBLK, R)
    return (live_tiles.astype(jnp.int32), first_source)


def draw_tile_source(key, part):
    live_tiles, first_source = tile_plan(key)
    key = jax.random.fold_in(key, 11)
    other_sources = jax.random.randint(key, (DBLK, R, K), 0, SRC)
    slot_number = jnp.arange(K, dtype=jnp.int32).reshape(1, 1, K)
    return jnp.where(slot_number == 0, first_source[:, :, None], other_sources).astype(jnp.int32)


def draw_counts(key, part):
    live_tiles, first_source = tile_plan(key)
    key = jax.random.fold_in(key, 23)
    subkeys = jax.random.split(key, 4)
    edge_rate = jax.random.randint(subkeys[0], (DBLK, R, 1, 1, 1), 2, 9)
    raw_draws = jax.random.randint(subkeys[1], (DBLK, R, K, BLOCK, BLOCK), 0, 12 * BLOCK)
    has_edge = raw_draws % (4 * BLOCK) < edge_rate
    edge_value = 1 + raw_draws // (4 * BLOCK)
    tile_counts = jnp.where(has_edge, edge_value, 0)
    forced_row = jax.random.randint(subkeys[2], (DBLK, R, K, 1, 1), 0, BLOCK)
    forced_col = jax.random.randint(subkeys[3], (DBLK, R, K, 1, 1), 0, BLOCK)
    row_index = jnp.arange(BLOCK, dtype=jnp.int32).reshape(1, 1, 1, BLOCK, 1)
    col_index = jnp.arange(BLOCK, dtype=jnp.int32).reshape(1, 1, 1, 1, BLOCK)
    forced_cell = (row_index == forced_row) & (col_index == forced_col)
    tile_counts = jnp.where(forced_cell, jnp.maximum(tile_counts, 1), tile_counts)
    slot_live = jnp.arange(K, dtype=jnp.int32).reshape(1, 1, K, 1, 1) < live_tiles[:, :, None, None, None]
    return jnp.where(slot_live, tile_counts, 0).astype(jnp.int32)


def with_ends(result, own_key, low, top_value):
    longest = result.shape.index(max(result.shape))
    spots = []
    for shift in (0, 1):
        where = [jax.random.randint(jax.random.fold_in(own_key, axis), (), 0, length) for axis, length in enumerate(result.shape)]
        where[longest] = (where[longest] + shift) % result.shape[longest]
        spots.append(tuple(where))
    return result.at[spots[0]].set(low).at[spots[1]].set(top_value)


def with_spikes(drawn, own_key, source, target, shards_of, factor):
    def block_of(axis_at):
        return (jnp.arange(drawn.shape[axis_at]) // (drawn.shape[axis_at] // shards_of)).reshape((-1,) + (1,) * (drawn.ndim - 1 - axis_at))

    first = jax.random.permutation(own_key, shards_of)[block_of(target)]
    other_side = (block_of(target) + shards_of // 2) % shards_of
    return jnp.where((block_of(source) == first) | (block_of(source) == other_side), factor * drawn, drawn)


def steps_of(rng, extent, pieces, low, high):
    gain = 1.0
    for axis_at, blocks in pieces:
        heights = jax.random.uniform(jax.random.fold_in(jax.random.fold_in(rng, 6), axis_at), (blocks,), jnp.float32, low / len(pieces), high / len(pieces))
        gain = gain * jnp.repeat(jnp.exp(heights), extent[axis_at] // blocks).reshape((-1,) + (1,) * (len(extent) - 1 - axis_at))
    return gain


def centred(rng, shape, deviation, limit, shards=(), held_as=jnp.bfloat16):
    result = deviation * jax.random.normal(rng, shape, jnp.float32)
    if shards:
        result = result * steps_of(rng, shape, shards, -0.22, 0.18)
    return jnp.clip(result, -limit, limit).astype(held_as)


def bell_draw_with(stream_key, extent, spread, limit, cuts, heavy, kind=jnp.bfloat16):
    result = spread * jax.random.normal(stream_key, extent, jnp.float32)
    if cuts:
        result = result * steps_of(stream_key, extent, cuts, -0.22, 0.18)
    return jnp.clip(with_spikes(result, jax.random.fold_in(stream_key, 3), *heavy), -limit, limit).astype(kind)


def setup_inputs(seed: int = 0) -> dict:
    splits = jax.random.split(jax.random.key(seed), 10)
    return {
        "features": centred(splits[0], (NODES, H_IN), 1.0, 6.0, ((0, 1024),)),
        "basis_weights": centred(splits[1], (B, H_IN, OUT), H_IN ** -0.5, 0.1875),
        "self_weight": centred(splits[2], (H_IN, OUT), H_IN ** -0.5, 0.1875),
        "coefficients": centred(splits[3], (R, B), 1.0, 4.0, (), jnp.float32),
        "counts": draw_counts(jax.random.fold_in(splits[9], 71), 0),
        "tile_source": draw_tile_source(jax.random.fold_in(splits[9], 71), 0),
        "send_rows": with_ends(jax.random.randint(splits[6], (DEVICES * N_GROUP, PEER_ROWS), 0, NBLK * BLOCK), jax.random.fold_in(splits[6], 1), 0, (NBLK * BLOCK) - 1).astype(jnp.int32),
        "edge_rows": with_ends(jax.random.randint(splits[7], (DEVICES * 2, HALO), 0, NBLK * BLOCK), jax.random.fold_in(splits[7], 1), 0, (NBLK * BLOCK) - 1).astype(jnp.int32),
        "cotangent": bell_draw_with(splits[8], (NODES, OUT), 1.0, 24.0, ((0, 1024),), (0, 1, 512, 6.0)),
    }


def reference(features, basis_weights, self_weight, coefficients, counts, tile_source, send_rows, edge_rows, cotangent):
    row_count = NBLK * BLOCK
    partitions = N_GROUP * N_OUTER
    send_table = send_rows.reshape(partitions, N_GROUP, PEER_ROWS)
    rim_table = edge_rows.reshape(partitions, 2, HALO)
    count_parts = counts.reshape(partitions, NBLK, R, K, BLOCK, BLOCK)
    tile_parts = tile_source.reshape(partitions, NBLK, R, K)
    peer_ids = jnp.arange(N_GROUP, dtype=jnp.int32)

    def one_part(grad_total, partition):
        group_index = partition // N_OUTER
        outer_index = partition % N_OUTER
        own_rows = lax.dynamic_slice_in_dim(features, partition * row_count, row_count, 0)
        senders = peer_ids * N_OUTER + outer_index
        picked = send_table[senders, group_index]
        incoming = features[(senders[:, None] * row_count + picked).reshape(-1)]
        lower_part = group_index * N_OUTER + (outer_index + N_OUTER - 1) % N_OUTER
        upper_part = group_index * N_OUTER + (outer_index + 1) % N_OUTER
        from_lower = features[lower_part * row_count + rim_table[lower_part, 1]]
        from_upper = features[upper_part * row_count + rim_table[upper_part, 0]]
        sources = jnp.concatenate([own_rows, incoming, from_lower, from_upper], 0).reshape(SRC, BLOCK, H_IN)
        tile_counts = count_parts[partition]
        chosen = sources[tile_parts[partition]]
        aggregate = jnp.einsum('drkij,drkjh->drih', tile_counts.astype(jnp.float32), chosen.astype(jnp.float32), precision=lax.Precision.HIGHEST)
        degree = lax.optimization_barrier(jnp.sum(tile_counts, axis=(2, 4)))
        normalized = aggregate / jnp.maximum(degree, 1).astype(jnp.float32)[..., None]
        mixed_list = []
        for basis_index in range(B):
            combined = coefficients[0, basis_index] * normalized[:, 0]
            for relation in range(1, R):
                combined = combined + coefficients[relation, basis_index] * normalized[:, relation]
            mixed_list.append(combined.reshape(row_count, H_IN))
        mixed_rows = jnp.stack(mixed_list).astype(jnp.bfloat16)
        layer_rows = jnp.dot(own_rows, self_weight, preferred_element_type=jnp.float32)
        for basis_index in range(B):
            layer_rows = layer_rows + jnp.dot(mixed_rows[basis_index], basis_weights[basis_index], preferred_element_type=jnp.float32)
        grad_rows = lax.dynamic_slice_in_dim(cotangent, partition * row_count, row_count, 0)
        grad_term = jnp.stack([jnp.dot(mixed_rows[basis_index].T, grad_rows, preferred_element_type=jnp.float32) for basis_index in range(B)])
        return (grad_total + grad_term, layer_rows.astype(jnp.bfloat16))
    grad_total, layer_parts = lax.scan(one_part, jnp.zeros((B, H_IN, OUT), jnp.float32), jnp.arange(partitions, dtype=jnp.int32))
    layer_out = layer_parts.reshape(NODES, OUT)
    basis_grad = grad_total / math.sqrt(NODES)
    return (layer_out, basis_grad)
```

```python
import functools
import math

import jax
import jax.numpy as jnp
from jax import lax
from jax.experimental import pallas as pl
from jax.experimental.pallas import tpu as pltpu
from jax.sharding import PartitionSpec as P

MESH = pl.DeviceIdType.MESH
CHUNKS = 4
F32 = jnp.float32
BF16 = jnp.bfloat16


def dot(a, b):
    return jnp.dot(a, b, preferred_element_type=F32)


def one_hot_of(column, width):
    lanes = lax.broadcasted_iota(jnp.int32, (column.shape[0], width), 1)
    return (lanes == column).astype(F32).astype(BF16)


def layer_kernel(
    sizes,
    features,
    basis_hbm,
    self_hbm,
    coefficients,
    counts_hbm,
    tile_source,
    send_rows,
    edge_rows,
    cotangent_hbm,
    layer_hbm,
    grad_out,
    counts,
    basis,
    own_weight,
    cotangent,
    cot_t,
    adjacency,
    weight_of,
    outgoing,
    arrived,
    mixed,
    layer,
    core_out,
    core_in,
    total,
    first_out,
    first_in,
    second_out,
    second_in,
    third_out,
    third_in,
    turned,
    load_sem,
    a_send,
    a_recv,
    c_send,
    c_recv,
    f_send,
    f_recv,
    s_send,
    s_recv,
    t_send,
    t_recv,
):
    groups, zs, xs, chunks, relations, slots, block = sizes
    g = lax.axis_index("group")
    o = lax.axis_index("outer")
    z, x = o // xs, o % xs
    core = g % 2
    rows, width = features.shape
    out_cols = cotangent.shape[1]
    peer_rows = send_rows.shape[1]
    blocks = rows // block
    pairs = blocks * relations
    part = width // chunks
    half = part // 2
    incoming = groups * peer_rows
    sources = adjacency.shape[1] // block
    z_rows = out_cols // zs
    tail = z_rows // xs

    barrier = pltpu.get_barrier_semaphore()

    def greet(group, outer):
        pl.semaphore_signal(
            barrier, inc=1, device_id={"group": group, "outer": outer}, device_id_type=MESH
        )

    def greet_group(i, carry):
        greet((g + i) % groups, o)
        return carry

    def greet_x(i, carry):
        greet(g, z * xs + (x + i) % xs)
        return carry

    def greet_z(i, carry):
        greet(g, ((z + i) % zs) * xs + x)
        return carry

    upper = (o + 1) % (zs * xs)
    lower = (o + zs * xs - 1) % (zs * xs)
    lax.fori_loop(1, groups, greet_group, 0)
    lax.fori_loop(1, xs, greet_x, 0)
    lax.fori_loop(1, zs, greet_z, 0)
    greet(g, upper)
    greet(g, lower)

    loads = [
        pltpu.make_async_copy(counts_hbm, counts, load_sem.at[0]),
        pltpu.make_async_copy(cotangent_hbm, cotangent, load_sem.at[1]),
        pltpu.make_async_copy(self_hbm, own_weight, load_sem.at[2]),
        pltpu.make_async_copy(basis_hbm, basis, load_sem.at[3]),
    ]
    for load in loads:
        load.start()

    slot_rows = jnp.broadcast_to(
        send_rows[...][:, None, :], (groups, peer_rows, peer_rows)
    ).reshape(incoming, peer_rows)
    at = lax.broadcasted_iota(jnp.int32, (incoming, peer_rows), 0) % peer_rows
    lane = lax.broadcasted_iota(jnp.int32, (incoming, peer_rows), 1)
    peer_index = jnp.sum(jnp.where(at == lane, slot_rows, 0), axis=1, keepdims=True)
    rim = edge_rows.shape[1]
    at = lax.broadcasted_iota(jnp.int32, (rim, rim), 0)
    lane = lax.broadcasted_iota(jnp.int32, (rim, rim), 1)
    rim_index = [
        jnp.sum(
            jnp.where(at == lane, jnp.broadcast_to(edge_rows[side : side + 1, :], (rim, rim)), 0),
            axis=1,
            keepdims=True,
        )
        for side in (0, 1)
    ]
    pick = one_hot_of(jnp.concatenate([peer_index] + rim_index, axis=0), rows)
    for c in range(chunks):
        outgoing[c] = dot(pick, features[:, c * part : (c + 1) * part]).astype(BF16)

    pl.semaphore_wait(barrier, groups - 1 + xs - 1 + zs - 1 + 2)

    own = pl.ds(pl.multiple_of(g * peer_rows, peer_rows), peer_rows)
    for c in range(chunks):

        def send_peer(i, carry, c=c):
            q = (g + i) % groups
            theirs = pl.ds(pl.multiple_of(q * peer_rows, peer_rows), peer_rows)
            pltpu.make_async_remote_copy(
                src_ref=outgoing.at[c, theirs],
                dst_ref=arrived.at[c, own],
                send_sem=a_send.at[c],
                recv_sem=a_recv.at[c],
                device_id={"group": q, "outer": o},
                device_id_type=MESH,
            ).start()
            return carry

        lax.fori_loop(1, groups, send_peer, 0)
        pltpu.make_async_copy(outgoing.at[c, own], arrived.at[c, own], a_recv.at[c]).start()
        for neighbour, start, land in (
            (lower, incoming, incoming + rim),
            (upper, incoming + rim, incoming),
        ):
            pltpu.make_async_remote_copy(
                src_ref=outgoing.at[c, start : start + rim],
                dst_ref=arrived.at[c, land : land + rim],
                send_sem=a_send.at[c],
                recv_sem=a_recv.at[c],
                device_id={"group": g, "outer": neighbour},
                device_id_type=MESH,
            ).start()

    loads[0].wait()

    def build(p, carry):
        t, r = p // relations, p % relations
        tiles = [counts[t, r, k].astype(F32) for k in range(slots)]
        named = [tile_source[t, r, k] for k in range(slots)]
        at_rows = pl.ds(pl.multiple_of(p * block, block), block)
        for s in range(sources):
            held = jnp.zeros((block, block), F32)
            for k in range(slots):
                held = held + jnp.where(named[k] == s, tiles[k], 0.0)
            adjacency[at_rows, s * block : (s + 1) * block] = held.astype(BF16)
        degree = jnp.sum(sum(tiles[1:], tiles[0]), axis=1, keepdims=True)
        inverse = 1.0 / jnp.maximum(degree, 1.0)
        for b in range(2):
            weight_of[b, at_rows] = jnp.broadcast_to(coefficients[r, b] * inverse, (block, block))
        return carry

    lax.fori_loop(0, pairs, build, 0)
    loads[1].wait()
    cot_t[...] = jnp.swapaxes(cotangent[...], 0, 1)

    def mix(c):
        cols = slice(c * part, (c + 1) * part)
        pltpu.make_async_copy(arrived.at[c], arrived.at[c], a_recv.at[c]).wait()
        for t in range(blocks):
            lo, hi = t * relations * block, (t + 1) * relations * block
            aggregate = dot(adjacency[lo:hi, :rows], features[:, cols]) + dot(
                adjacency[lo:hi, rows:], arrived[c]
            )
            for b in range(2):
                for u in range(part // 128):
                    lanes = slice(u * 128, (u + 1) * 128)
                    value = weight_of[b, lo : lo + block] * aggregate[:block, lanes]
                    for r in range(1, relations):
                        value = value + (
                            weight_of[b, lo + r * block : lo + (r + 1) * block]
                            * aggregate[r * block : (r + 1) * block, lanes]
                        )
                    mixed[b, c, t * block : (t + 1) * block, lanes] = value.astype(BF16)
        core_out[c] = dot(cot_t[...], mixed[1 - core, c]).astype(BF16)
        pltpu.make_async_remote_copy(
            src_ref=core_out.at[c],
            dst_ref=core_in.at[c],
            send_sem=c_send.at[c],
            recv_sem=c_recv.at[c],
            device_id={"group": g + 1 - 2 * core, "outer": o},
            device_id_type=MESH,
        ).start()
        total[c] = dot(cot_t[...], mixed[core, c])

    def along(kind, i):
        if kind == 0:
            there = (z + i) % zs
            return there, there * xs + x
        there = (x + i) % xs
        return there, z * xs + there

    def spread_first(c):
        pltpu.make_async_copy(core_in.at[c], core_in.at[c], c_recv.at[c]).wait()
        whole = total[c] + core_in[c].astype(F32)
        by_z = whole[:, :half]
        by_x = whole[:, half:]
        by_x = jnp.concatenate(
            [
                by_x[zi * z_rows + xi * tail : zi * z_rows + (xi + 1) * tail]
                for xi in range(xs)
                for zi in range(zs)
            ],
            axis=0,
        )
        for kind, value in ((0, by_z), (1, by_x)):
            total[c, :, kind * half : (kind + 1) * half] = value
            first_out[c, kind] = value.astype(BF16)
        for kind, count in ((0, zs), (1, xs)):
            size = out_cols // count

            def send(i, carry, kind=kind, size=size):
                there, outer = along(kind, i)
                pltpu.make_async_remote_copy(
                    src_ref=first_out.at[c, kind, pl.ds(pl.multiple_of(there * size, size), size)],
                    dst_ref=first_in.at[c, kind, i - 1],
                    send_sem=f_send.at[c, kind],
                    recv_sem=f_recv.at[c, kind],
                    device_id={"group": g, "outer": outer},
                    device_id_type=MESH,
                ).start()
                return carry

            lax.fori_loop(1, count, send, 0)

    def spread_second(c):
        for kind, count, mine in ((0, zs, z), (1, xs, x)):
            size = out_cols // count
            landed = first_in.at[c, kind]
            pltpu.make_async_copy(landed, landed, f_recv.at[c, kind]).wait()
            held = total[
                c, pl.ds(pl.multiple_of(mine * size, size), size), kind * half : (kind + 1) * half
            ]
            for i in range(count - 1):
                held = held + first_in[c, kind, i].astype(F32)
            second_out[c, kind] = held
        for kind, count in ((0, xs), (1, zs)):

            def send(i, carry, kind=kind):
                there, outer = along(1 - kind, i)
                pltpu.make_async_remote_copy(
                    src_ref=second_out.at[c, kind, pl.ds(pl.multiple_of(there * tail, tail), tail)],
                    dst_ref=second_in.at[c, kind, i - 1],
                    send_sem=s_send.at[c, kind],
                    recv_sem=s_recv.at[c, kind],
                    device_id={"group": g, "outer": outer},
                    device_id_type=MESH,
                ).start()
                return carry

            lax.fori_loop(1, count, send, 0)

    def spread_third(c):
        for kind, count, mine in ((0, xs, x), (1, zs, z)):
            landed = second_in.at[c, kind]
            pltpu.make_async_copy(landed, landed, s_recv.at[c, kind]).wait()
            held = second_out[c, kind, pl.ds(pl.multiple_of(mine * tail, tail), tail)]
            for i in range(count - 1):
                held = held + second_in[c, kind, i]
            for u in range(half // 128):
                y = (c * part + kind * half) // 128 + u
                third_out[y] = held[:, u * 128 : (u + 1) * 128]
                for q in (2 * y, 2 * y + 1):

                    @pl.when(q != g)
                    def _(y=y, q=q):
                        pltpu.make_async_remote_copy(
                            src_ref=third_out.at[y],
                            dst_ref=third_in.at[g],
                            send_sem=t_send,
                            recv_sem=t_recv,
                            device_id={"group": q, "outer": o},
                            device_id_type=MESH,
                        ).start()

                    @pl.when(q == g)
                    def _(y=y):
                        pltpu.make_async_copy(third_out.at[y], third_in.at[g], t_recv).start()

    for step in range(chunks):
        mix(step)
        if step >= 1:
            spread_second(step - 1)
        spread_first(step)
        if step >= 2:
            spread_third(step - 2)

    loads[2].wait()
    loads[3].wait()
    value = dot(features[...], own_weight[...])
    for b in range(2):
        for c in range(chunks):
            value = value + dot(mixed[b, c], basis[b, c * part : (c + 1) * part])
    layer[...] = value.astype(BF16)
    store = pltpu.make_async_copy(layer, layer_hbm, load_sem.at[4])
    store.start()

    if chunks >= 2:
        spread_third(chunks - 2)
    spread_second(chunks - 1)
    spread_third(chunks - 1)

    pltpu.make_async_copy(third_in, third_in, t_recv).wait()
    scale = 1.0 / math.sqrt(rows * groups * zs * xs)
    for b in range(2):
        value = third_in[b]
        for y in range(1, groups // 2):
            value = value + third_in[2 * y + b]
        turned[b] = jnp.swapaxes(value * scale, 0, 1)
        wide = width // groups
        grad_out[b] = turned[b, pl.ds(pl.multiple_of(core * wide, wide), wide)]

    store.wait()
    for c in range(chunks):
        sent = outgoing.at[c, : outgoing.shape[1] - peer_rows]
        pltpu.make_async_copy(sent, sent, a_send.at[c]).wait()
        pltpu.make_async_copy(core_out.at[c], core_out.at[c], c_send.at[c]).wait()
        for kind in (0, 1):
            pltpu.make_async_copy(
                first_in.at[c, kind], first_in.at[c, kind], f_send.at[c, kind]
            ).wait()
            pltpu.make_async_copy(
                second_in.at[c, kind], second_in.at[c, kind], s_send.at[c, kind]
            ).wait()
    sent = third_in.at[: groups - 1]
    pltpu.make_async_copy(sent, sent, t_send).wait()


def shards(
    mesh_sizes,
    features,
    basis_weights,
    self_weight,
    coefficients,
    counts,
    tile_source,
    send_rows,
    edge_rows,
    cotangent,
):
    groups, zs, xs = mesh_sizes
    rows, width = features.shape
    out_cols = cotangent.shape[1]
    blocks, relations, slots, block, _ = counts.shape
    chunks = min(CHUNKS, width // 256)
    part = width // chunks
    half = part // 2
    peers = groups * send_rows.shape[1]
    arriving = peers + 2 * edge_rows.shape[1]
    pairs = blocks * relations
    sizes = (groups, zs, xs, chunks, relations, slots, block)
    z_rows = out_cols // zs
    tail = z_rows // xs
    vmem = pl.BlockSpec(memory_space=pltpu.VMEM)
    smem = pl.BlockSpec(memory_space=pltpu.SMEM)
    anywhere = pl.BlockSpec(memory_space=pl.ANY)
    dma = pltpu.SemaphoreType.DMA
    return pl.pallas_call(
        functools.partial(layer_kernel, sizes),
        out_shape=(
            jax.ShapeDtypeStruct((rows, out_cols), BF16),
            jax.ShapeDtypeStruct((2, width // groups, tail), F32),
        ),
        in_specs=[vmem, anywhere, anywhere, smem, anywhere, smem, vmem, vmem, anywhere],
        out_specs=(anywhere, vmem),
        scratch_shapes=[
            pltpu.VMEM(counts.shape, jnp.int32),
            pltpu.VMEM(basis_weights.shape, BF16),
            pltpu.VMEM(self_weight.shape, BF16),
            pltpu.VMEM((rows, out_cols), BF16),
            pltpu.VMEM((out_cols, rows), BF16),
            pltpu.VMEM((pairs * block, rows + arriving), BF16),
            pltpu.VMEM((2, pairs * block, block), F32),
            pltpu.VMEM((chunks, arriving, part), BF16),
            pltpu.VMEM((chunks, arriving, part), BF16),
            pltpu.VMEM((2, chunks, rows, part), BF16),
            pltpu.VMEM((rows, out_cols), BF16),
            pltpu.VMEM((chunks, out_cols, part), BF16),
            pltpu.VMEM((chunks, out_cols, part), BF16),
            pltpu.VMEM((chunks, out_cols, part), F32),
            pltpu.VMEM((chunks, 2, out_cols, half), BF16),
            pltpu.VMEM((chunks, 2, zs - 1, z_rows, half), BF16),
            pltpu.VMEM((chunks, 2, z_rows, half), F32),
            pltpu.VMEM((chunks, 2, zs - 1, tail, half), F32),
            pltpu.VMEM((groups // 2, tail, 128), F32),
            pltpu.VMEM((groups, tail, 128), F32),
            pltpu.VMEM((2, 128, tail), F32),
            dma((5,)),
            dma((chunks,)),
            dma((chunks,)),
            dma((chunks,)),
            dma((chunks,)),
            dma((chunks, 2)),
            dma((chunks, 2)),
            dma((chunks, 2)),
            dma((chunks, 2)),
            dma,
            dma,
        ],
        compiler_params=pltpu.CompilerParams(
            collective_id=0, has_side_effects=True, vmem_limit_bytes=56 * 1024 * 1024
        ),
        cost_estimate=pl.CostEstimate(
            flops=3 * 10**9, bytes_accessed=6 * 10**6, transcendentals=0
        ),
        name="graph_layer",
    )(
        features,
        basis_weights,
        self_weight,
        coefficients,
        counts,
        tile_source,
        send_rows,
        edge_rows,
        cotangent,
    )


def solution(mesh):
    groups, outers = mesh.shape["group"], mesh.shape["outer"]
    side = math.isqrt(outers)
    return jax.shard_map(
        functools.partial(shards, (groups, side, side)),
        mesh=mesh,
        in_specs=(
            P(("group", "outer"), None),
            P(),
            P(),
            P(),
            P(("group", "outer"), None, None, None, None),
            P(("group", "outer"), None, None),
            P(("group", "outer"), None),
            P(("group", "outer"), None),
            P(("group", "outer"), None),
        ),
        out_specs=(P(("group", "outer"), None), P(None, "group", "outer")),
        check_vma=False,
    )
```

```python
import functools
import math

import jax
import jax.numpy as jnp
from jax import lax
from jax.experimental import pallas as pl
from jax.experimental.pallas import tpu as pltpu
from jax.sharding import PartitionSpec as P

MESH = pl.DeviceIdType.MESH
CHUNKS = 4
AHEAD = 3
F32 = jnp.float32
BF16 = jnp.bfloat16


def dot(a, b):
    return jnp.dot(a, b, preferred_element_type=F32)


def one_hot_of(column, width):
    lanes = lax.broadcasted_iota(jnp.int32, (column.shape[0], width), 1)
    return (lanes == column).astype(F32).astype(BF16)


def layer_kernel(
    sizes,
    features_hbm,
    basis_hbm,
    self_hbm,
    coefficients,
    counts_hbm,
    tile_source,
    send_rows,
    edge_rows,
    cotangent_hbm,
    layer_hbm,
    grad_out,
    features,
    counts,
    basis,
    own_weight,
    cotangent,
    cot_t,
    adjacency,
    weight_of,
    outgoing,
    arrived,
    mixed,
    layer,
    core_out,
    core_in,
    total,
    first_out,
    first_in,
    second_out,
    second_in,
    third_out,
    third_in,
    load_sem,
    a_send,
    a_recv,
    c_send,
    c_recv,
    f_send,
    f_recv,
    s_send,
    s_recv,
    t_send,
    t_recv,
):
    groups, zs, xs, chunks, relations, slots, block = sizes
    g = lax.axis_index("group")
    o = lax.axis_index("outer")
    z, x = o // xs, o % xs
    core = g % 2
    rows, width = features.shape
    out_cols = cotangent.shape[1]
    peer_rows = send_rows.shape[1]
    blocks = rows // block
    pairs = blocks * relations
    part = width // chunks
    half = part // 2
    incoming = groups * peer_rows
    sources = adjacency.shape[1] // block
    z_rows = out_cols // zs
    tail = z_rows // xs

    barrier = pltpu.get_barrier_semaphore()

    def greet(group, outer):
        pl.semaphore_signal(
            barrier, inc=1, device_id={"group": group, "outer": outer}, device_id_type=MESH
        )

    def greet_group(i, carry):
        greet((g + i) % groups, o)
        return carry

    def greet_x(i, carry):
        greet(g, z * xs + (x + i) % xs)
        return carry

    def greet_z(i, carry):
        greet(g, ((z + i) % zs) * xs + x)
        return carry

    upper = (o + 1) % (zs * xs)
    lower = (o + zs * xs - 1) % (zs * xs)
    lax.fori_loop(1, groups, greet_group, 0)
    lax.fori_loop(1, xs, greet_x, 0)
    lax.fori_loop(1, zs, greet_z, 0)
    greet(g, upper)
    greet(g, lower)

    loads = [
        pltpu.make_async_copy(counts_hbm, counts, load_sem.at[0]),
        pltpu.make_async_copy(cotangent_hbm, cotangent, load_sem.at[1]),
        pltpu.make_async_copy(self_hbm, own_weight, load_sem.at[2]),
        pltpu.make_async_copy(basis_hbm, basis, load_sem.at[3]),
        pltpu.make_async_copy(features_hbm, features, load_sem.at[5]),
    ]
    for load in loads[-1:] + loads[:-1]:
        load.start()

    slot_rows = jnp.broadcast_to(
        send_rows[...][:, None, :], (groups, peer_rows, peer_rows)
    ).reshape(incoming, peer_rows)
    at = lax.broadcasted_iota(jnp.int32, (incoming, peer_rows), 0) % peer_rows
    lane = lax.broadcasted_iota(jnp.int32, (incoming, peer_rows), 1)
    peer_index = jnp.sum(jnp.where(at == lane, slot_rows, 0), axis=1, keepdims=True)
    rim = edge_rows.shape[1]
    at = lax.broadcasted_iota(jnp.int32, (rim, rim), 0)
    lane = lax.broadcasted_iota(jnp.int32, (rim, rim), 1)
    rim_index = [
        jnp.sum(
            jnp.where(at == lane, jnp.broadcast_to(edge_rows[side : side + 1, :], (rim, rim)), 0),
            axis=1,
            keepdims=True,
        )
        for side in (0, 1)
    ]
    pick = one_hot_of(jnp.concatenate([peer_index] + rim_index, axis=0), rows)
    loads[-1].wait()
    outgoing[0] = dot(pick, features[:, :part]).astype(BF16)
    pl.semaphore_wait(barrier, groups - 1 + xs - 1 + zs - 1 + 2)

    own = pl.ds(pl.multiple_of(g * peer_rows, peer_rows), peer_rows)
    def exchange(c):
        def send_peer(i, carry):
            q = (g + i) % groups
            theirs = pl.ds(pl.multiple_of(q * peer_rows, peer_rows), peer_rows)
            pltpu.make_async_remote_copy(
                src_ref=outgoing.at[c, theirs],
                dst_ref=arrived.at[c, own],
                send_sem=a_send.at[c],
                recv_sem=a_recv.at[c],
                device_id={"group": q, "outer": o},
                device_id_type=MESH,
            ).start()
            return carry

        lax.fori_loop(1, groups, send_peer, 0)
        pltpu.make_async_copy(outgoing.at[c, own], arrived.at[c, own], a_recv.at[c]).start()
        for neighbour, start, land in (
            (lower, incoming, incoming + rim),
            (upper, incoming + rim, incoming),
        ):
            pltpu.make_async_remote_copy(
                src_ref=outgoing.at[c, start : start + rim],
                dst_ref=arrived.at[c, land : land + rim],
                send_sem=a_send.at[c],
                recv_sem=a_recv.at[c],
                device_id={"group": g, "outer": neighbour},
                device_id_type=MESH,
            ).start()

    for c in range(chunks):
        if c >= 1:
            outgoing[c] = dot(pick, features[:, c * part : (c + 1) * part]).astype(BF16)
        if c < AHEAD:
            exchange(c)

    loads[0].wait()

    def build(p, carry):
        t, r = p // relations, p % relations
        tiles = [counts[t, r, k].astype(F32) for k in range(slots)]
        row = tile_source[r, pl.ds(t, 1)]
        named = [jnp.broadcast_to(row[:, k : k + 1], (block, block)) for k in range(slots)]
        at_rows = pl.ds(pl.multiple_of(p * block, block), block)
        for s in range(sources):
            held = jnp.zeros((block, block), F32)
            for k in range(slots):
                held = held + jnp.where(named[k] == s, tiles[k], 0.0)
            adjacency[at_rows, s * block : (s + 1) * block] = held.astype(BF16)
        degree = jnp.sum(sum(tiles[1:], tiles[0]), axis=1, keepdims=True)
        inverse = 1.0 / jnp.maximum(degree, 1.0)
        for b in range(2):
            lanes = lax.broadcasted_iota(jnp.int32, (1, relations), 1)
            gain = jnp.sum(
                jnp.where(lanes == r, coefficients[b : b + 1], 0.0), axis=1, keepdims=True
            )
            weight_of[b, at_rows] = jnp.broadcast_to(gain * inverse, (block, block))
        return carry

    lax.fori_loop(0, pairs, build, 0)
    loads[1].wait()
    cot_t[...] = jnp.swapaxes(cotangent[...], 0, 1)

    def mix(c):
        cols = slice(c * part, (c + 1) * part)
        pltpu.make_async_copy(arrived.at[c], arrived.at[c], a_recv.at[c]).wait()
        if c + AHEAD < chunks:
            exchange(c + AHEAD)
        for t in range(blocks):
            lo, hi = t * relations * block, (t + 1) * relations * block
            aggregate = dot(adjacency[lo:hi, :rows], features[:, cols]) + dot(
                adjacency[lo:hi, rows:], arrived[c]
            )
            for b in range(2):
                for u in range(part // 128):
                    lanes = slice(u * 128, (u + 1) * 128)
                    value = weight_of[b, lo : lo + block] * aggregate[:block, lanes]
                    for r in range(1, relations):
                        value = value + (
                            weight_of[b, lo + r * block : lo + (r + 1) * block]
                            * aggregate[r * block : (r + 1) * block, lanes]
                        )
                    mixed[b, c, t * block : (t + 1) * block, lanes] = value.astype(BF16)
        core_out[c] = dot(cot_t[...], mixed[1 - core, c]).astype(BF16)
        pltpu.make_async_remote_copy(
            src_ref=core_out.at[c],
            dst_ref=core_in.at[c],
            send_sem=c_send.at[c],
            recv_sem=c_recv.at[c],
            device_id={"group": g + 1 - 2 * core, "outer": o},
            device_id_type=MESH,
        ).start()
        total[c] = dot(cot_t[...], mixed[core, c])

    def along(kind, i):
        if kind == 0:
            there = (z + i) % zs
            return there, there * xs + x
        there = (x + i) % xs
        return there, z * xs + there

    def spread_first(c):
        pltpu.make_async_copy(core_in.at[c], core_in.at[c], c_recv.at[c]).wait()
        whole = total[c] + core_in[c].astype(F32)
        by_z = whole[:, :half]
        by_x = whole[:, half:]
        by_x = jnp.concatenate(
            [
                by_x[zi * z_rows + xi * tail : zi * z_rows + (xi + 1) * tail]
                for xi in range(xs)
                for zi in range(zs)
            ],
            axis=0,
        )
        for kind, count, value in ((0, zs, by_z), (1, xs, by_x)):
            first_out[c, kind] = value.astype(BF16)
            total[c, :, kind * half : (kind + 1) * half] = value
            size = out_cols // count

            def send(i, carry, kind=kind, size=size):
                there, outer = along(kind, i)
                pltpu.make_async_remote_copy(
                    src_ref=first_out.at[c, kind, pl.ds(pl.multiple_of(there * size, size), size)],
                    dst_ref=first_in.at[c, kind, i - 1],
                    send_sem=f_send.at[c, kind],
                    recv_sem=f_recv.at[c, kind],
                    device_id={"group": g, "outer": outer},
                    device_id_type=MESH,
                ).start()
                return carry

            lax.fori_loop(1, count, send, 0)

    def spread_second(c):
        for kind, count, mine in ((0, zs, z), (1, xs, x)):
            size = out_cols // count
            landed = first_in.at[c, kind]
            pltpu.make_async_copy(landed, landed, f_recv.at[c, kind]).wait()
            held = total[
                c, pl.ds(pl.multiple_of(mine * size, size), size), kind * half : (kind + 1) * half
            ]
            for i in range(count - 1):
                held = held + first_in[c, kind, i].astype(F32)
            second_out[c, kind] = held
        for kind, count in ((0, xs), (1, zs)):

            def send(i, carry, kind=kind):
                there, outer = along(1 - kind, i)
                pltpu.make_async_remote_copy(
                    src_ref=second_out.at[c, kind, pl.ds(pl.multiple_of(there * tail, tail), tail)],
                    dst_ref=second_in.at[c, kind, i - 1],
                    send_sem=s_send.at[c, kind],
                    recv_sem=s_recv.at[c, kind],
                    device_id={"group": g, "outer": outer},
                    device_id_type=MESH,
                ).start()
                return carry

            lax.fori_loop(1, count, send, 0)

    def spread_third(c):
        for kind, count, mine in ((0, xs, x), (1, zs, z)):
            landed = second_in.at[c, kind]
            pltpu.make_async_copy(landed, landed, s_recv.at[c, kind]).wait()
            held = second_out[c, kind, pl.ds(pl.multiple_of(mine * tail, tail), tail)]
            for i in range(count - 1):
                held = held + second_in[c, kind, i]
            for u in range(half // 128):
                y = (c * part + kind * half) // 128 + u
                third_out[y] = held[:, u * 128 : (u + 1) * 128]
                for q in (2 * y, 2 * y + 1):

                    @pl.when(q != g)
                    def _(y=y, q=q):
                        pltpu.make_async_remote_copy(
                            src_ref=third_out.at[y],
                            dst_ref=third_in.at[g],
                            send_sem=t_send,
                            recv_sem=t_recv,
                            device_id={"group": q, "outer": o},
                            device_id_type=MESH,
                        ).start()

                    @pl.when(q == g)
                    def _(y=y):
                        pltpu.make_async_copy(third_out.at[y], third_in.at[g], t_recv).start()

    for step in range(chunks):
        mix(step)
        spread_first(step)
        if step >= 2:
            spread_second(step - 2)
        if step >= 3:
            spread_third(step - 3)

    loads[2].wait()
    loads[3].wait()
    value = dot(features[...], own_weight[...])
    for b in range(2):
        for c in range(chunks):
            value = value + dot(mixed[b, c], basis[b, c * part : (c + 1) * part])
    layer[...] = value.astype(BF16)
    store = pltpu.make_async_copy(layer, layer_hbm, load_sem.at[4])
    store.start()

    if chunks >= 2:
        spread_second(chunks - 2)
    if chunks >= 3:
        spread_third(chunks - 3)
    spread_second(chunks - 1)
    if chunks >= 2:
        spread_third(chunks - 2)
    spread_third(chunks - 1)

    pltpu.make_async_copy(third_in, third_in, t_recv).wait()
    scale = 1.0 / math.sqrt(rows * groups * zs * xs)
    for b in range(2):
        value = third_in[b]
        for y in range(1, groups // 2):
            value = value + third_in[2 * y + b]
        value = value * scale
        wide = width // groups
        grad_out[b] = jnp.where(core == 0, value[:, :wide], value[:, wide:])

    store.wait()
    for c in range(chunks):
        sent = outgoing.at[c, : outgoing.shape[1] - peer_rows]
        pltpu.make_async_copy(sent, sent, a_send.at[c]).wait()
        pltpu.make_async_copy(core_out.at[c], core_out.at[c], c_send.at[c]).wait()
        for kind in (0, 1):
            pltpu.make_async_copy(
                first_in.at[c, kind], first_in.at[c, kind], f_send.at[c, kind]
            ).wait()
            pltpu.make_async_copy(
                second_in.at[c, kind], second_in.at[c, kind], s_send.at[c, kind]
            ).wait()
    sent = third_in.at[: groups - 1]
    pltpu.make_async_copy(sent, sent, t_send).wait()


def shards(
    mesh_sizes,
    features,
    basis_weights,
    self_weight,
    coefficients,
    counts,
    tile_source,
    send_rows,
    edge_rows,
    cotangent,
):
    groups, zs, xs = mesh_sizes
    rows, width = features.shape
    out_cols = cotangent.shape[1]
    blocks, relations, slots, block, _ = counts.shape
    chunks = min(CHUNKS, width // 256)
    part = width // chunks
    half = part // 2
    peers = groups * send_rows.shape[1]
    arriving = peers + 2 * edge_rows.shape[1]
    pairs = blocks * relations
    sizes = (groups, zs, xs, chunks, relations, slots, block)
    z_rows = out_cols // zs
    tail = z_rows // xs
    vmem = pl.BlockSpec(memory_space=pltpu.VMEM)
    anywhere = pl.BlockSpec(memory_space=pl.ANY)
    dma = pltpu.SemaphoreType.DMA
    layer_out, grad = pl.pallas_call(
        functools.partial(layer_kernel, sizes),
        out_shape=(
            jax.ShapeDtypeStruct((rows, out_cols), BF16),
            jax.ShapeDtypeStruct((2, tail, width // groups), F32),
        ),
        in_specs=[anywhere, anywhere, anywhere, vmem, anywhere, vmem, vmem, vmem, anywhere],
        out_specs=(anywhere, vmem),
        scratch_shapes=[
            pltpu.VMEM(features.shape, BF16),
            pltpu.VMEM(counts.shape, jnp.int32),
            pltpu.VMEM(basis_weights.shape, BF16),
            pltpu.VMEM(self_weight.shape, BF16),
            pltpu.VMEM((rows, out_cols), BF16),
            pltpu.VMEM((out_cols, rows), BF16),
            pltpu.VMEM((pairs * block, rows + arriving), BF16),
            pltpu.VMEM((2, pairs * block, block), F32),
            pltpu.VMEM((chunks, arriving, part), BF16),
            pltpu.VMEM((chunks, arriving, part), BF16),
            pltpu.VMEM((2, chunks, rows, part), BF16),
            pltpu.VMEM((rows, out_cols), BF16),
            pltpu.VMEM((chunks, out_cols, part), BF16),
            pltpu.VMEM((chunks, out_cols, part), BF16),
            pltpu.VMEM((chunks, out_cols, part), F32),
            pltpu.VMEM((chunks, 2, out_cols, half), BF16),
            pltpu.VMEM((chunks, 2, zs - 1, z_rows, half), BF16),
            pltpu.VMEM((chunks, 2, z_rows, half), F32),
            pltpu.VMEM((chunks, 2, zs - 1, tail, half), F32),
            pltpu.VMEM((groups // 2, tail, 128), F32),
            pltpu.VMEM((groups, tail, 128), F32),
            dma((6,)),
            dma((chunks,)),
            dma((chunks,)),
            dma((chunks,)),
            dma((chunks,)),
            dma((chunks, 2)),
            dma((chunks, 2)),
            dma((chunks, 2)),
            dma((chunks, 2)),
            dma,
            dma,
        ],
        compiler_params=pltpu.CompilerParams(
            collective_id=0, has_side_effects=True, vmem_limit_bytes=56 * 1024 * 1024
        ),
        cost_estimate=pl.CostEstimate(
            flops=3 * 10**9, bytes_accessed=6 * 10**6, transcendentals=0
        ),
        name="graph_layer",
    )(
        features,
        basis_weights,
        self_weight,
        coefficients.T,
        counts,
        tile_source.transpose(1, 0, 2),
        send_rows,
        edge_rows,
        cotangent,
    )
    return layer_out, grad.transpose(0, 2, 1)


def solution(mesh):
    groups, outers = mesh.shape["group"], mesh.shape["outer"]
    side = math.isqrt(outers)
    return jax.shard_map(
        functools.partial(shards, (groups, side, side)),
        mesh=mesh,
        in_specs=(
            P(("group", "outer"), None),
            P(),
            P(),
            P(),
            P(("group", "outer"), None, None, None, None),
            P(("group", "outer"), None, None),
            P(("group", "outer"), None),
            P(("group", "outer"), None),
            P(("group", "outer"), None),
        ),
        out_specs=(P(("group", "outer"), None), P(None, "group", "outer")),
        check_vma=False,
    )
```

```python
import functools
import math

import jax
import jax.numpy as jnp
from jax import lax
from jax.experimental import pallas as pl
from jax.experimental.pallas import tpu as pltpu
from jax.sharding import PartitionSpec as P

MESH = pl.DeviceIdType.MESH
CHUNKS = 4
AHEAD = 3
F32 = jnp.float32
BF16 = jnp.bfloat16


def dot(a, b):
    return jnp.dot(a, b, preferred_element_type=F32)


def one_hot_of(column, width):
    lanes = lax.broadcasted_iota(jnp.int32, (column.shape[0], width), 1)
    return (lanes == column).astype(F32).astype(BF16)


def layer_kernel(
    sizes,
    features_hbm,
    basis_hbm,
    self_hbm,
    coefficients_hbm,
    counts_hbm,
    tile_source_hbm,
    send_rows_hbm,
    edge_rows_hbm,
    cotangent_hbm,
    layer_hbm,
    grad_out,
    features,
    coefficients,
    tile_source,
    send_rows,
    edge_rows,
    counts,
    basis,
    own_weight,
    cotangent,
    cot_t,
    adjacency,
    weight_of,
    outgoing,
    arrived,
    mixed,
    layer,
    core_out,
    core_in,
    total,
    first_out,
    first_in,
    second_out,
    second_in,
    third_out,
    third_in,
    load_sem,
    a_send,
    a_recv,
    c_send,
    c_recv,
    f_send,
    f_recv,
    s_send,
    s_recv,
    t_send,
    t_recv,
):
    groups, zs, xs, chunks, relations, slots, block = sizes
    g = lax.axis_index("group")
    o = lax.axis_index("outer")
    z, x = lax.div(o, xs), lax.rem(o, xs)
    core = lax.rem(g, 2)
    rows, width = features.shape
    out_cols = cotangent.shape[1]
    peer_rows = send_rows.shape[1]
    blocks = rows // block
    pairs = blocks * relations
    part = width // chunks
    half = part // 2
    incoming = groups * peer_rows
    sources = adjacency.shape[1] // block
    z_rows = out_cols // zs
    tail = z_rows // xs

    def load(source, target, i):
        copy = pltpu.make_async_copy(source, target, load_sem.at[i])
        copy.start()
        return copy

    send_load = load(send_rows_hbm, send_rows, 6)
    edge_load = load(edge_rows_hbm, edge_rows, 7)
    feature_load = load(features_hbm, features, 5)
    gain_load = load(coefficients_hbm, coefficients, 8)
    source_load = load(tile_source_hbm, tile_source, 9)
    counts_load = load(counts_hbm, counts, 0)
    cotangent_load = load(cotangent_hbm, cotangent, 1)
    own_load = load(self_hbm, own_weight, 2)
    basis_load = load(basis_hbm, basis, 3)

    barrier = pltpu.get_barrier_semaphore()

    def greet(group, outer):
        pl.semaphore_signal(
            barrier, inc=1, device_id={"group": group, "outer": outer}, device_id_type=MESH
        )

    def greet_group(i, carry):
        greet(lax.rem(g + i, groups), o)
        return carry

    def greet_x(i, carry):
        greet(g, z * xs + lax.rem(x + i, xs))
        return carry

    def greet_z(i, carry):
        greet(g, lax.rem(z + i, zs) * xs + x)
        return carry

    upper = lax.rem(o + 1, zs * xs)
    lower = lax.rem(o + zs * xs - 1, zs * xs)
    lax.fori_loop(1, groups, greet_group, 0)
    lax.fori_loop(1, xs, greet_x, 0)
    lax.fori_loop(1, zs, greet_z, 0)
    greet(g, upper)
    greet(g, lower)

    send_load.wait()
    edge_load.wait()
    slot_rows = jnp.broadcast_to(
        send_rows[...][:, None, :], (groups, peer_rows, peer_rows)
    ).reshape(incoming, peer_rows)
    at = lax.broadcasted_iota(jnp.int32, (incoming, peer_rows), 0) % peer_rows
    lane = lax.broadcasted_iota(jnp.int32, (incoming, peer_rows), 1)
    peer_index = jnp.sum(jnp.where(at == lane, slot_rows, 0), axis=1, keepdims=True)
    rim = edge_rows.shape[1]
    at = lax.broadcasted_iota(jnp.int32, (rim, rim), 0)
    lane = lax.broadcasted_iota(jnp.int32, (rim, rim), 1)
    rim_index = [
        jnp.sum(
            jnp.where(at == lane, jnp.broadcast_to(edge_rows[side : side + 1, :], (rim, rim)), 0),
            axis=1,
            keepdims=True,
        )
        for side in (0, 1)
    ]
    pick = one_hot_of(jnp.concatenate([peer_index] + rim_index, axis=0), rows)
    feature_load.wait()
    outgoing[0] = dot(pick, features[:, :part]).astype(BF16)
    pl.semaphore_wait(barrier, groups - 1 + xs - 1 + zs - 1 + 2)

    own = pl.ds(pl.multiple_of(g * peer_rows, peer_rows), peer_rows)
    def exchange(c):
        def send_peer(i, carry):
            q = lax.rem(g + i, groups)
            theirs = pl.ds(pl.multiple_of(q * peer_rows, peer_rows), peer_rows)
            pltpu.make_async_remote_copy(
                src_ref=outgoing.at[c, theirs],
                dst_ref=arrived.at[c, own],
                send_sem=a_send.at[c],
                recv_sem=a_recv.at[c],
                device_id={"group": q, "outer": o},
                device_id_type=MESH,
            ).start()
            return carry

        lax.fori_loop(1, groups, send_peer, 0)
        pltpu.make_async_copy(outgoing.at[c, own], arrived.at[c, own], a_recv.at[c]).start()
        for neighbour, start, land in (
            (lower, incoming, incoming + rim),
            (upper, incoming + rim, incoming),
        ):
            pltpu.make_async_remote_copy(
                src_ref=outgoing.at[c, start : start + rim],
                dst_ref=arrived.at[c, land : land + rim],
                send_sem=a_send.at[c],
                recv_sem=a_recv.at[c],
                device_id={"group": g, "outer": neighbour},
                device_id_type=MESH,
            ).start()

    for c in range(chunks):
        if c >= 1:
            outgoing[c] = dot(pick, features[:, c * part : (c + 1) * part]).astype(BF16)
        if c < AHEAD:
            exchange(c)

    gain_load.wait()
    source_load.wait()
    counts_load.wait()

    def build(p, carry):
        t, r = lax.div(p, relations), lax.rem(p, relations)
        tiles = [counts[t, r, k].astype(F32) for k in range(slots)]
        row = tile_source[r, pl.ds(t, 1)]
        named = [jnp.broadcast_to(row[:, k : k + 1], (block, block)) for k in range(slots)]
        at_rows = pl.ds(pl.multiple_of(p * block, block), block)
        for s in range(sources):
            held = jnp.zeros((block, block), F32)
            for k in range(slots):
                held = held + jnp.where(named[k] == s, tiles[k], 0.0)
            adjacency[at_rows, s * block : (s + 1) * block] = held.astype(BF16)
        degree = jnp.sum(sum(tiles[1:], tiles[0]), axis=1, keepdims=True)
        inverse = 1.0 / jnp.maximum(degree, 1.0)
        for b in range(2):
            lanes = lax.broadcasted_iota(jnp.int32, (1, relations), 1)
            gain = jnp.sum(
                jnp.where(lanes == r, coefficients[b : b + 1], 0.0), axis=1, keepdims=True
            )
            weight_of[b, at_rows] = jnp.broadcast_to(gain * inverse, (block, block))
        return carry

    lax.fori_loop(0, pairs, build, 0)
    cotangent_load.wait()
    cot_t[...] = jnp.swapaxes(cotangent[...], 0, 1)

    def mix(c):
        cols = slice(c * part, (c + 1) * part)
        pltpu.make_async_copy(arrived.at[c], arrived.at[c], a_recv.at[c]).wait()
        if c + AHEAD < chunks:
            exchange(c + AHEAD)
        for t in range(blocks):
            lo, hi = t * relations * block, (t + 1) * relations * block
            aggregate = dot(adjacency[lo:hi, :rows], features[:, cols]) + dot(
                adjacency[lo:hi, rows:], arrived[c]
            )
            for b in range(2):
                for u in range(part // 128):
                    lanes = slice(u * 128, (u + 1) * 128)
                    value = weight_of[b, lo : lo + block] * aggregate[:block, lanes]
                    for r in range(1, relations):
                        value = value + (
                            weight_of[b, lo + r * block : lo + (r + 1) * block]
                            * aggregate[r * block : (r + 1) * block, lanes]
                        )
                    mixed[b, c, t * block : (t + 1) * block, lanes] = value.astype(BF16)
        core_out[c] = dot(cot_t[...], mixed[1 - core, c]).astype(BF16)
        pltpu.make_async_remote_copy(
            src_ref=core_out.at[c],
            dst_ref=core_in.at[c],
            send_sem=c_send.at[c],
            recv_sem=c_recv.at[c],
            device_id={"group": g + 1 - 2 * core, "outer": o},
            device_id_type=MESH,
        ).start()
        total[c] = dot(cot_t[...], mixed[core, c])

    def along(kind, i):
        if kind == 0:
            there = lax.rem(z + i, zs)
            return there, there * xs + x
        there = lax.rem(x + i, xs)
        return there, z * xs + there

    def spread_first(c):
        pltpu.make_async_copy(core_in.at[c], core_in.at[c], c_recv.at[c]).wait()
        whole = total[c] + core_in[c].astype(F32)
        by_z = whole[:, :half]
        by_x = whole[:, half:]
        by_x = jnp.concatenate(
            [
                by_x[zi * z_rows + xi * tail : zi * z_rows + (xi + 1) * tail]
                for xi in range(xs)
                for zi in range(zs)
            ],
            axis=0,
        )
        for kind, count, value in ((0, zs, by_z), (1, xs, by_x)):
            first_out[c, kind] = value.astype(BF16)
            total[c, :, kind * half : (kind + 1) * half] = value
            size = out_cols // count

            def send(i, carry, kind=kind, size=size):
                there, outer = along(kind, i)
                pltpu.make_async_remote_copy(
                    src_ref=first_out.at[c, kind, pl.ds(pl.multiple_of(there * size, size), size)],
                    dst_ref=first_in.at[c, kind, i - 1],
                    send_sem=f_send.at[c, kind],
                    recv_sem=f_recv.at[c, kind],
                    device_id={"group": g, "outer": outer},
                    device_id_type=MESH,
                ).start()
                return carry

            lax.fori_loop(1, count, send, 0)

    def spread_second(c):
        for kind, count, mine in ((0, zs, z), (1, xs, x)):
            size = out_cols // count
            landed = first_in.at[c, kind]
            pltpu.make_async_copy(landed, landed, f_recv.at[c, kind]).wait()
            held = total[
                c, pl.ds(pl.multiple_of(mine * size, size), size), kind * half : (kind + 1) * half
            ]
            for i in range(count - 1):
                held = held + first_in[c, kind, i].astype(F32)
            second_out[c, kind] = held

            def send(i, carry, kind=kind):
                there, outer = along(1 - kind, i)
                pltpu.make_async_remote_copy(
                    src_ref=second_out.at[c, kind, pl.ds(pl.multiple_of(there * tail, tail), tail)],
                    dst_ref=second_in.at[c, kind, i - 1],
                    send_sem=s_send.at[c, kind],
                    recv_sem=s_recv.at[c, kind],
                    device_id={"group": g, "outer": outer},
                    device_id_type=MESH,
                ).start()
                return carry

            lax.fori_loop(1, (xs, zs)[kind], send, 0)

    def spread_third(c):
        for kind, count, mine in ((0, xs, x), (1, zs, z)):
            landed = second_in.at[c, kind]
            pltpu.make_async_copy(landed, landed, s_recv.at[c, kind]).wait()
            held = second_out[c, kind, pl.ds(pl.multiple_of(mine * tail, tail), tail)]
            for i in range(count - 1):
                held = held + second_in[c, kind, i]
            for u in range(half // 128):
                y = (c * part + kind * half) // 128 + u
                third_out[y] = held[:, u * 128 : (u + 1) * 128]
                for q in (2 * y, 2 * y + 1):

                    @pl.when(q != g)
                    def _(y=y, q=q):
                        pltpu.make_async_remote_copy(
                            src_ref=third_out.at[y],
                            dst_ref=third_in.at[g],
                            send_sem=t_send,
                            recv_sem=t_recv,
                            device_id={"group": q, "outer": o},
                            device_id_type=MESH,
                        ).start()

                    @pl.when(q == g)
                    def _(y=y):
                        pltpu.make_async_copy(third_out.at[y], third_in.at[g], t_recv).start()

    for step in range(chunks):
        mix(step)
        spread_first(step)
        if step >= 2:
            spread_second(step - 2)
        if step >= 3:
            spread_third(step - 3)

    own_load.wait()
    basis_load.wait()
    value = dot(features[...], own_weight[...])
    for b in range(2):
        for c in range(chunks):
            value = value + dot(mixed[b, c], basis[b, c * part : (c + 1) * part])
    layer[...] = value.astype(BF16)
    store = pltpu.make_async_copy(layer, layer_hbm, load_sem.at[4])
    store.start()

    if chunks >= 2:
        spread_second(chunks - 2)
    if chunks >= 3:
        spread_third(chunks - 3)
    spread_second(chunks - 1)
    if chunks >= 2:
        spread_third(chunks - 2)
    spread_third(chunks - 1)

    pltpu.make_async_copy(third_in, third_in, t_recv).wait()
    scale = 1.0 / math.sqrt(rows * groups * zs * xs)
    for b in range(2):
        value = third_in[b]
        for y in range(1, groups // 2):
            value = value + third_in[2 * y + b]
        value = value * scale
        wide = width // groups
        grad_out[b] = jnp.where(core == 0, value[:, :wide], value[:, wide:])

    store.wait()
    for c in range(chunks):
        sent = outgoing.at[c, : outgoing.shape[1] - peer_rows]
        pltpu.make_async_copy(sent, sent, a_send.at[c]).wait()
        pltpu.make_async_copy(core_out.at[c], core_out.at[c], c_send.at[c]).wait()
        for kind in (0, 1):
            pltpu.make_async_copy(
                first_in.at[c, kind], first_in.at[c, kind], f_send.at[c, kind]
            ).wait()
            pltpu.make_async_copy(
                second_in.at[c, kind], second_in.at[c, kind], s_send.at[c, kind]
            ).wait()
    sent = third_in.at[: groups - 1]
    pltpu.make_async_copy(sent, sent, t_send).wait()


def hand_over(layer, grad, layer_out, grad_out, layer_held, grad_held, sem):
    arriving = [
        pltpu.make_async_copy(layer, layer_held, sem.at[0]),
        pltpu.make_async_copy(grad, grad_held, sem.at[1]),
    ]
    leaving = [
        pltpu.make_async_copy(layer_held, layer_out, sem.at[2]),
        pltpu.make_async_copy(grad_held, grad_out, sem.at[3]),
    ]
    for copy in arriving:
        copy.start()
    for copy, then in zip(arriving, leaving):
        copy.wait()
        then.start()
    for copy in leaving:
        copy.wait()


def shards(
    mesh_sizes,
    features,
    basis_weights,
    self_weight,
    coefficients,
    counts,
    tile_source,
    send_rows,
    edge_rows,
    cotangent,
):
    groups, zs, xs = mesh_sizes
    rows, width = features.shape
    out_cols = cotangent.shape[1]
    blocks, relations, slots, block, _ = counts.shape
    chunks = min(CHUNKS, width // 256)
    part = width // chunks
    half = part // 2
    peers = groups * send_rows.shape[1]
    arriving = peers + 2 * edge_rows.shape[1]
    pairs = blocks * relations
    sizes = (groups, zs, xs, chunks, relations, slots, block)
    z_rows = out_cols // zs
    tail = z_rows // xs
    vmem = pl.BlockSpec(memory_space=pltpu.VMEM)
    anywhere = pl.BlockSpec(memory_space=pl.ANY)
    dma = pltpu.SemaphoreType.DMA
    layer_out, grad = pl.pallas_call(
        functools.partial(layer_kernel, sizes),
        out_shape=(
            jax.ShapeDtypeStruct((rows, out_cols), BF16),
            jax.ShapeDtypeStruct((2, tail, width // groups), F32),
        ),
        in_specs=[anywhere] * 9,
        out_specs=(anywhere, vmem),
        scratch_shapes=[
            pltpu.VMEM(features.shape, BF16),
            pltpu.VMEM(coefficients.shape[::-1], F32),
            pltpu.VMEM((relations, blocks, slots), jnp.int32),
            pltpu.VMEM(send_rows.shape, jnp.int32),
            pltpu.VMEM(edge_rows.shape, jnp.int32),
            pltpu.VMEM(counts.shape, jnp.int32),
            pltpu.VMEM(basis_weights.shape, BF16),
            pltpu.VMEM(self_weight.shape, BF16),
            pltpu.VMEM((rows, out_cols), BF16),
            pltpu.VMEM((out_cols, rows), BF16),
            pltpu.VMEM((pairs * block, rows + arriving), BF16),
            pltpu.VMEM((2, pairs * block, block), F32),
            pltpu.VMEM((chunks, arriving, part), BF16),
            pltpu.VMEM((chunks, arriving, part), BF16),
            pltpu.VMEM((2, chunks, rows, part), BF16),
            pltpu.VMEM((rows, out_cols), BF16),
            pltpu.VMEM((chunks, out_cols, part), BF16),
            pltpu.VMEM((chunks, out_cols, part), BF16),
            pltpu.VMEM((chunks, out_cols, part), F32),
            pltpu.VMEM((chunks, 2, out_cols, half), BF16),
            pltpu.VMEM((chunks, 2, zs - 1, z_rows, half), BF16),
            pltpu.VMEM((chunks, 2, z_rows, half), F32),
            pltpu.VMEM((chunks, 2, zs - 1, tail, half), F32),
            pltpu.VMEM((groups // 2, tail, 128), F32),
            pltpu.VMEM((groups, tail, 128), F32),
            dma((10,)),
            dma((chunks,)),
            dma((chunks,)),
            dma((chunks,)),
            dma((chunks,)),
            dma((chunks, 2)),
            dma((chunks, 2)),
            dma((chunks, 2)),
            dma((chunks, 2)),
            dma,
            dma,
        ],
        compiler_params=pltpu.CompilerParams(
            collective_id=0, has_side_effects=True, vmem_limit_bytes=56 * 1024 * 1024
        ),
        cost_estimate=pl.CostEstimate(
            flops=3 * 10**9, bytes_accessed=6 * 10**6, transcendentals=0
        ),
        name="graph_layer",
    )(
        features,
        basis_weights,
        self_weight,
        coefficients.T,
        counts,
        tile_source.transpose(1, 0, 2),
        send_rows,
        edge_rows,
        cotangent,
    )
    layer_out, grad = pl.pallas_call(
        hand_over,
        out_shape=(
            jax.ShapeDtypeStruct(layer_out.shape, layer_out.dtype),
            jax.ShapeDtypeStruct(grad.shape, grad.dtype),
        ),
        in_specs=[anywhere, anywhere],
        out_specs=(anywhere, anywhere),
        scratch_shapes=[
            pltpu.VMEM(layer_out.shape, layer_out.dtype),
            pltpu.VMEM(grad.shape, grad.dtype),
            dma((4,)),
        ],
        compiler_params=pltpu.CompilerParams(vmem_limit_bytes=56 * 1024 * 1024),
        name="hand_over",
    )(layer_out, grad)
    return layer_out, grad.transpose(0, 2, 1)


def solution(mesh):
    groups, outers = mesh.shape["group"], mesh.shape["outer"]
    side = math.isqrt(outers)
    return jax.shard_map(
        functools.partial(shards, (groups, side, side)),
        mesh=mesh,
        in_specs=(
            P(("group", "outer"), None),
            P(),
            P(),
            P(),
            P(("group", "outer"), None, None, None, None),
            P(("group", "outer"), None, None),
            P(("group", "outer"), None),
            P(("group", "outer"), None),
            P(("group", "outer"), None),
        ),
        out_specs=(P(("group", "outer"), None), P(None, "group", "outer")),
        check_vma=False,
    )
```

```python
import functools
import math

import jax
import jax.numpy as jnp
from jax import lax
from jax.experimental import pallas as pl
from jax.experimental.pallas import tpu as pltpu
from jax.sharding import PartitionSpec as P

MESH = pl.DeviceIdType.MESH
CHUNKS = 4
AHEAD = 3
F32 = jnp.float32
BF16 = jnp.bfloat16


def dot(a, b):
    return jnp.dot(a, b, preferred_element_type=F32)


def one_hot_of(column, width):
    lanes = lax.broadcasted_iota(jnp.int32, (column.shape[0], width), 1)
    return (lanes == column).astype(F32).astype(BF16)


def layer_kernel(
    sizes,
    features_hbm,
    basis_hbm,
    self_hbm,
    coefficients_hbm,
    counts_hbm,
    tile_source_hbm,
    send_rows_hbm,
    edge_rows_hbm,
    cotangent_hbm,
    layer,
    grad_out,
    features,
    coefficients,
    tile_source,
    send_rows,
    edge_rows,
    counts,
    basis,
    own_weight,
    cotangent,
    cot_t,
    adjacency,
    weight_of,
    outgoing,
    arrived,
    mixed,
    core_out,
    core_in,
    total,
    first_out,
    first_in,
    second_out,
    second_in,
    third_out,
    third_in,
    load_sem,
    a_send,
    a_recv,
    c_send,
    c_recv,
    f_send,
    f_recv,
    s_send,
    s_recv,
    t_send,
    t_recv,
):
    groups, zs, xs, chunks, relations, slots, block = sizes
    g = lax.axis_index("group")
    o = lax.axis_index("outer")
    z, x = lax.div(o, xs), lax.rem(o, xs)
    core = lax.rem(g, 2)
    rows, width = features.shape
    out_cols = cotangent.shape[1]
    peer_rows = send_rows.shape[1]
    blocks = rows // block
    pairs = blocks * relations
    part = width // chunks
    half = part // 2
    incoming = groups * peer_rows
    sources = adjacency.shape[1] // block
    z_rows = out_cols // zs
    tail = z_rows // xs

    def load(source, target, i):
        copy = pltpu.make_async_copy(source, target, load_sem.at[i])
        copy.start()
        return copy

    send_load = load(send_rows_hbm, send_rows, 6)
    edge_load = load(edge_rows_hbm, edge_rows, 7)
    feature_load = load(features_hbm, features, 5)
    gain_load = load(coefficients_hbm, coefficients, 8)
    source_load = load(tile_source_hbm, tile_source, 9)

    barrier = pltpu.get_barrier_semaphore()

    def greet(group, outer):
        pl.semaphore_signal(
            barrier, inc=1, device_id={"group": group, "outer": outer}, device_id_type=MESH
        )

    def greet_group(i, carry):
        greet(lax.rem(g + i, groups), o)
        return carry

    def greet_x(i, carry):
        greet(g, z * xs + lax.rem(x + i, xs))
        return carry

    def greet_z(i, carry):
        greet(g, lax.rem(z + i, zs) * xs + x)
        return carry

    upper = lax.rem(o + 1, zs * xs)
    lower = lax.rem(o + zs * xs - 1, zs * xs)
    lax.fori_loop(1, groups, greet_group, 0)
    lax.fori_loop(1, xs, greet_x, 0)
    lax.fori_loop(1, zs, greet_z, 0)
    greet(g, upper)
    greet(g, lower)

    send_load.wait()
    edge_load.wait()
    slot_rows = jnp.broadcast_to(
        send_rows[...][:, None, :], (groups, peer_rows, peer_rows)
    ).reshape(incoming, peer_rows)
    at = lax.broadcasted_iota(jnp.int32, (incoming, peer_rows), 0) % peer_rows
    lane = lax.broadcasted_iota(jnp.int32, (incoming, peer_rows), 1)
    peer_index = jnp.sum(jnp.where(at == lane, slot_rows, 0), axis=1, keepdims=True)
    rim = edge_rows.shape[1]
    at = lax.broadcasted_iota(jnp.int32, (rim, rim), 0)
    lane = lax.broadcasted_iota(jnp.int32, (rim, rim), 1)
    rim_index = [
        jnp.sum(
            jnp.where(at == lane, jnp.broadcast_to(edge_rows[side : side + 1, :], (rim, rim)), 0),
            axis=1,
            keepdims=True,
        )
        for side in (0, 1)
    ]
    pick = one_hot_of(jnp.concatenate([peer_index] + rim_index, axis=0), rows)
    feature_load.wait()
    counts_load = load(counts_hbm, counts, 0)
    cotangent_load = load(cotangent_hbm, cotangent, 1)
    outgoing[0] = dot(pick, features[:, :part]).astype(BF16)
    pl.semaphore_wait(barrier, groups - 1 + xs - 1 + zs - 1 + 2)

    own = pl.ds(pl.multiple_of(g * peer_rows, peer_rows), peer_rows)
    def exchange(c):
        def send_peer(i, carry):
            q = lax.rem(g + i, groups)
            theirs = pl.ds(pl.multiple_of(q * peer_rows, peer_rows), peer_rows)
            pltpu.make_async_remote_copy(
                src_ref=outgoing.at[c, theirs],
                dst_ref=arrived.at[c, own],
                send_sem=a_send.at[c],
                recv_sem=a_recv.at[c],
                device_id={"group": q, "outer": o},
                device_id_type=MESH,
            ).start()
            return carry

        lax.fori_loop(1, groups, send_peer, 0)
        pltpu.make_async_copy(outgoing.at[c, own], arrived.at[c, own], a_recv.at[c]).start()
        for neighbour, start, land in (
            (lower, incoming, incoming + rim),
            (upper, incoming + rim, incoming),
        ):
            pltpu.make_async_remote_copy(
                src_ref=outgoing.at[c, start : start + rim],
                dst_ref=arrived.at[c, land : land + rim],
                send_sem=a_send.at[c],
                recv_sem=a_recv.at[c],
                device_id={"group": g, "outer": neighbour},
                device_id_type=MESH,
            ).start()

    for c in range(chunks):
        if c >= 1:
            outgoing[c] = dot(pick, features[:, c * part : (c + 1) * part]).astype(BF16)
        if c < AHEAD:
            exchange(c)

    own_load = load(self_hbm, own_weight, 2)
    basis_load = load(basis_hbm, basis, 3)

    gain_load.wait()
    source_load.wait()
    counts_load.wait()

    def build(p, carry):
        t, r = lax.div(p, relations), lax.rem(p, relations)
        tiles = [counts[t, r, k].astype(F32) for k in range(slots)]
        row = tile_source[r, pl.ds(t, 1)]
        named = [jnp.broadcast_to(row[:, k : k + 1], (block, block)) for k in range(slots)]
        at_rows = pl.ds(pl.multiple_of(p * block, block), block)
        for s in range(sources):
            held = jnp.zeros((block, block), F32)
            for k in range(slots):
                held = held + jnp.where(named[k] == s, tiles[k], 0.0)
            adjacency[at_rows, s * block : (s + 1) * block] = held.astype(BF16)
        degree = jnp.sum(sum(tiles[1:], tiles[0]), axis=1, keepdims=True)
        inverse = 1.0 / jnp.maximum(degree, 1.0)
        for b in range(2):
            lanes = lax.broadcasted_iota(jnp.int32, (1, relations), 1)
            gain = jnp.sum(
                jnp.where(lanes == r, coefficients[b : b + 1], 0.0), axis=1, keepdims=True
            )
            weight_of[b, at_rows] = jnp.broadcast_to(gain * inverse, (block, block))
        return carry

    lax.fori_loop(0, pairs, build, 0)
    cotangent_load.wait()
    cot_t[...] = jnp.swapaxes(cotangent[...], 0, 1)

    def mix(c):
        cols = slice(c * part, (c + 1) * part)
        pltpu.make_async_copy(arrived.at[c], arrived.at[c], a_recv.at[c]).wait()
        if c + AHEAD < chunks:
            exchange(c + AHEAD)
        for t in range(blocks):
            lo, hi = t * relations * block, (t + 1) * relations * block
            aggregate = dot(adjacency[lo:hi, :rows], features[:, cols]) + dot(
                adjacency[lo:hi, rows:], arrived[c]
            )
            for b in range(2):
                for u in range(part // 128):
                    lanes = slice(u * 128, (u + 1) * 128)
                    value = weight_of[b, lo : lo + block] * aggregate[:block, lanes]
                    for r in range(1, relations):
                        value = value + (
                            weight_of[b, lo + r * block : lo + (r + 1) * block]
                            * aggregate[r * block : (r + 1) * block, lanes]
                        )
                    mixed[b, c, t * block : (t + 1) * block, lanes] = value.astype(BF16)
        core_out[c] = dot(cot_t[...], mixed[1 - core, c]).astype(BF16)
        pltpu.make_async_remote_copy(
            src_ref=core_out.at[c],
            dst_ref=core_in.at[c],
            send_sem=c_send.at[c],
            recv_sem=c_recv.at[c],
            device_id={"group": g + 1 - 2 * core, "outer": o},
            device_id_type=MESH,
        ).start()
        total[c] = dot(cot_t[...], mixed[core, c])

    def along(kind, i):
        if kind == 0:
            there = lax.rem(z + i, zs)
            return there, there * xs + x
        there = lax.rem(x + i, xs)
        return there, z * xs + there

    def spread_first(c):
        pltpu.make_async_copy(core_in.at[c], core_in.at[c], c_recv.at[c]).wait()
        whole = total[c] + core_in[c].astype(F32)
        by_z = whole[:, :half]
        by_x = whole[:, half:]
        by_x = jnp.concatenate(
            [
                by_x[zi * z_rows + xi * tail : zi * z_rows + (xi + 1) * tail]
                for xi in range(xs)
                for zi in range(zs)
            ],
            axis=0,
        )
        for kind, count, value in ((0, zs, by_z), (1, xs, by_x)):
            first_out[c, kind] = value.astype(BF16)
            total[c, :, kind * half : (kind + 1) * half] = value
            size = out_cols // count

            def send(i, carry, kind=kind, size=size):
                there, outer = along(kind, i)
                pltpu.make_async_remote_copy(
                    src_ref=first_out.at[c, kind, pl.ds(pl.multiple_of(there * size, size), size)],
                    dst_ref=first_in.at[c, kind, i - 1],
                    send_sem=f_send.at[c, kind],
                    recv_sem=f_recv.at[c, kind],
                    device_id={"group": g, "outer": outer},
                    device_id_type=MESH,
                ).start()
                return carry

            lax.fori_loop(1, count, send, 0)

    def spread_second(c):
        for kind, count, mine in ((0, zs, z), (1, xs, x)):
            size = out_cols // count
            landed = first_in.at[c, kind]
            pltpu.make_async_copy(landed, landed, f_recv.at[c, kind]).wait()
            held = total[
                c, pl.ds(pl.multiple_of(mine * size, size), size), kind * half : (kind + 1) * half
            ]
            for i in range(count - 1):
                held = held + first_in[c, kind, i].astype(F32)
            second_out[c, kind] = held

            def send(i, carry, kind=kind):
                there, outer = along(1 - kind, i)
                pltpu.make_async_remote_copy(
                    src_ref=second_out.at[c, kind, pl.ds(pl.multiple_of(there * tail, tail), tail)],
                    dst_ref=second_in.at[c, kind, i - 1],
                    send_sem=s_send.at[c, kind],
                    recv_sem=s_recv.at[c, kind],
                    device_id={"group": g, "outer": outer},
                    device_id_type=MESH,
                ).start()
                return carry

            lax.fori_loop(1, (xs, zs)[kind], send, 0)

    def spread_third(c):
        for kind, count, mine in ((0, xs, x), (1, zs, z)):
            landed = second_in.at[c, kind]
            pltpu.make_async_copy(landed, landed, s_recv.at[c, kind]).wait()
            held = second_out[c, kind, pl.ds(pl.multiple_of(mine * tail, tail), tail)]
            for i in range(count - 1):
                held = held + second_in[c, kind, i]
            for u in range(half // 128):
                y = (c * part + kind * half) // 128 + u
                third_out[y] = held[:, u * 128 : (u + 1) * 128]
                for q in (2 * y, 2 * y + 1):

                    @pl.when(q != g)
                    def _(y=y, q=q):
                        pltpu.make_async_remote_copy(
                            src_ref=third_out.at[y],
                            dst_ref=third_in.at[g],
                            send_sem=t_send,
                            recv_sem=t_recv,
                            device_id={"group": q, "outer": o},
                            device_id_type=MESH,
                        ).start()

                    @pl.when(q == g)
                    def _(y=y):
                        pltpu.make_async_copy(third_out.at[y], third_in.at[g], t_recv).start()

    for step in range(chunks):
        mix(step)
        spread_first(step)
        if step >= 2:
            spread_second(step - 2)
        if step >= 3:
            spread_third(step - 3)

    own_load.wait()
    basis_load.wait()
    value = dot(features[...], own_weight[...])
    for b in range(2):
        for c in range(chunks):
            value = value + dot(mixed[b, c], basis[b, c * part : (c + 1) * part])
    layer[...] = value.astype(BF16)

    if chunks >= 2:
        spread_second(chunks - 2)
    if chunks >= 3:
        spread_third(chunks - 3)
    spread_second(chunks - 1)
    if chunks >= 2:
        spread_third(chunks - 2)
    spread_third(chunks - 1)

    pltpu.make_async_copy(third_in, third_in, t_recv).wait()
    scale = 1.0 / math.sqrt(rows * groups * zs * xs)
    for b in range(2):
        value = third_in[b]
        for y in range(1, groups // 2):
            value = value + third_in[2 * y + b]
        value = value * scale
        wide = width // groups
        grad_out[b] = jnp.where(core == 0, value[:, :wide], value[:, wide:])

    for c in range(chunks):
        sent = outgoing.at[c, : outgoing.shape[1] - peer_rows]
        pltpu.make_async_copy(sent, sent, a_send.at[c]).wait()
        pltpu.make_async_copy(core_out.at[c], core_out.at[c], c_send.at[c]).wait()
        for kind in (0, 1):
            pltpu.make_async_copy(
                first_in.at[c, kind], first_in.at[c, kind], f_send.at[c, kind]
            ).wait()
            pltpu.make_async_copy(
                second_in.at[c, kind], second_in.at[c, kind], s_send.at[c, kind]
            ).wait()
    sent = third_in.at[: groups - 1]
    pltpu.make_async_copy(sent, sent, t_send).wait()


def hand_over(layer, grad, layer_out, grad_out, sem):
    copies = [
        pltpu.make_async_copy(layer, layer_out, sem.at[0]),
        pltpu.make_async_copy(grad, grad_out, sem.at[1]),
    ]
    for copy in copies:
        copy.start()
    for copy in copies:
        copy.wait()


def shards(
    mesh_sizes,
    features,
    basis_weights,
    self_weight,
    coefficients,
    counts,
    tile_source,
    send_rows,
    edge_rows,
    cotangent,
):
    groups, zs, xs = mesh_sizes
    rows, width = features.shape
    out_cols = cotangent.shape[1]
    blocks, relations, slots, block, _ = counts.shape
    chunks = min(CHUNKS, width // 256)
    part = width // chunks
    half = part // 2
    peers = groups * send_rows.shape[1]
    arriving = peers + 2 * edge_rows.shape[1]
    pairs = blocks * relations
    sizes = (groups, zs, xs, chunks, relations, slots, block)
    z_rows = out_cols // zs
    tail = z_rows // xs
    vmem = pl.BlockSpec(memory_space=pltpu.VMEM)
    anywhere = pl.BlockSpec(memory_space=pl.ANY)
    dma = pltpu.SemaphoreType.DMA
    layer_out, grad = pl.pallas_call(
        functools.partial(layer_kernel, sizes),
        out_shape=(
            pltpu.VMEM((rows, out_cols), BF16),
            pltpu.VMEM((2, tail, width // groups), F32),
        ),
        in_specs=[anywhere] * 9,
        out_specs=(vmem, vmem),
        scratch_shapes=[
            pltpu.VMEM(features.shape, BF16),
            pltpu.VMEM(coefficients.shape[::-1], F32),
            pltpu.VMEM((relations, blocks, slots), jnp.int32),
            pltpu.VMEM(send_rows.shape, jnp.int32),
            pltpu.VMEM(edge_rows.shape, jnp.int32),
            pltpu.VMEM(counts.shape, jnp.int32),
            pltpu.VMEM(basis_weights.shape, BF16),
            pltpu.VMEM(self_weight.shape, BF16),
            pltpu.VMEM((rows, out_cols), BF16),
            pltpu.VMEM((out_cols, rows), BF16),
            pltpu.VMEM((pairs * block, rows + arriving), BF16),
            pltpu.VMEM((2, pairs * block, block), F32),
            pltpu.VMEM((chunks, arriving, part), BF16),
            pltpu.VMEM((chunks, arriving, part), BF16),
            pltpu.VMEM((2, chunks, rows, part), BF16),
            pltpu.VMEM((chunks, out_cols, part), BF16),
            pltpu.VMEM((chunks, out_cols, part), BF16),
            pltpu.VMEM((chunks, out_cols, part), F32),
            pltpu.VMEM((chunks, 2, out_cols, half), BF16),
            pltpu.VMEM((chunks, 2, zs - 1, z_rows, half), BF16),
            pltpu.VMEM((chunks, 2, z_rows, half), F32),
            pltpu.VMEM((chunks, 2, zs - 1, tail, half), F32),
            pltpu.VMEM((groups // 2, tail, 128), F32),
            pltpu.VMEM((groups, tail, 128), F32),
            dma((10,)),
            dma((chunks,)),
            dma((chunks,)),
            dma((chunks,)),
            dma((chunks,)),
            dma((chunks, 2)),
            dma((chunks, 2)),
            dma((chunks, 2)),
            dma((chunks, 2)),
            dma,
            dma,
        ],
        compiler_params=pltpu.CompilerParams(
            collective_id=0, has_side_effects=True, vmem_limit_bytes=56 * 1024 * 1024
        ),
        cost_estimate=pl.CostEstimate(
            flops=3 * 10**9, bytes_accessed=6 * 10**6, transcendentals=0
        ),
        name="graph_layer",
    )(
        features,
        basis_weights,
        self_weight,
        coefficients.T,
        counts,
        tile_source.transpose(1, 0, 2),
        send_rows,
        edge_rows,
        cotangent,
    )
    layer_out, grad = pl.pallas_call(
        hand_over,
        out_shape=(
            jax.ShapeDtypeStruct(layer_out.shape, layer_out.dtype),
            jax.ShapeDtypeStruct(grad.shape, grad.dtype),
        ),
        in_specs=[vmem, vmem],
        out_specs=(anywhere, anywhere),
        scratch_shapes=[dma((2,))],
        compiler_params=pltpu.CompilerParams(vmem_limit_bytes=4 * 1024 * 1024),
        name="hand_over",
    )(layer_out, grad)
    return layer_out, grad.transpose(0, 2, 1)


def solution(mesh):
    groups, outers = mesh.shape["group"], mesh.shape["outer"]
    side = math.isqrt(outers)
    return jax.shard_map(
        functools.partial(shards, (groups, side, side)),
        mesh=mesh,
        in_specs=(
            P(("group", "outer"), None),
            P(),
            P(),
            P(),
            P(("group", "outer"), None, None, None, None),
            P(("group", "outer"), None, None),
            P(("group", "outer"), None),
            P(("group", "outer"), None),
            P(("group", "outer"), None),
        ),
        out_specs=(P(("group", "outer"), None), P(None, "group", "outer")),
        check_vma=False,
    )
```

```python
import functools
import math

import jax
import jax.numpy as jnp
from jax import lax
from jax.experimental import pallas as pl
from jax.experimental.pallas import tpu as pltpu
from jax.sharding import PartitionSpec as P

MESH = pl.DeviceIdType.MESH
CHUNKS = 4
AHEAD = 3
F32 = jnp.float32
BF16 = jnp.bfloat16


def dot(a, b):
    return jnp.dot(a, b, preferred_element_type=F32)


def one_hot_of(column, width):
    lanes = lax.broadcasted_iota(jnp.int32, (column.shape[0], width), 1)
    return (lanes == column).astype(F32).astype(BF16)


def layer_kernel(
    sizes,
    features_hbm,
    basis_hbm,
    self_hbm,
    coefficients_hbm,
    counts_hbm,
    tile_source_hbm,
    send_rows_hbm,
    edge_rows_hbm,
    cotangent_hbm,
    layer,
    grad_out,
    features,
    coefficients,
    tile_source,
    send_rows,
    edge_rows,
    counts,
    basis,
    own_weight,
    cotangent,
    cot_t,
    adjacency,
    weight_of,
    outgoing,
    arrived,
    mixed,
    core_out,
    core_in,
    total,
    first_out,
    first_in,
    second_out,
    second_in,
    third_out,
    third_in,
    load_sem,
    a_send,
    a_recv,
    c_send,
    c_recv,
    f_send,
    f_recv,
    s_send,
    s_recv,
    t_send,
    t_recv,
):
    groups, zs, xs, chunks, relations, slots, block = sizes
    g = lax.axis_index("group")
    o = lax.axis_index("outer")
    z, x = lax.div(o, xs), lax.rem(o, xs)
    core = lax.rem(g, 2)
    rows, width = features.shape
    out_cols = cotangent.shape[1]
    peer_rows = send_rows.shape[1]
    blocks = rows // block
    pairs = blocks * relations
    part = width // chunks
    half = part // 2
    incoming = groups * peer_rows
    sources = adjacency.shape[1] // block
    z_rows = out_cols // zs
    tail = z_rows // xs

    def load(source, target, i):
        copy = pltpu.make_async_copy(source, target, load_sem.at[i])
        copy.start()
        return copy

    send_load = load(send_rows_hbm, send_rows, 6)
    edge_load = load(edge_rows_hbm, edge_rows, 7)
    feature_load = load(features_hbm, features, 5)
    gain_load = load(coefficients_hbm, coefficients, 8)
    source_load = load(tile_source_hbm, tile_source, 9)

    barrier = pltpu.get_barrier_semaphore()

    def greet(group, outer):
        pl.semaphore_signal(
            barrier, inc=1, device_id={"group": group, "outer": outer}, device_id_type=MESH
        )

    def greet_group(i, carry):
        greet(lax.rem(g + i, groups), o)
        return carry

    def greet_x(i, carry):
        greet(g, z * xs + lax.rem(x + i, xs))
        return carry

    def greet_z(i, carry):
        greet(g, lax.rem(z + i, zs) * xs + x)
        return carry

    upper = lax.rem(o + 1, zs * xs)
    lower = lax.rem(o + zs * xs - 1, zs * xs)
    lax.fori_loop(1, groups, greet_group, 0)
    lax.fori_loop(1, xs, greet_x, 0)
    lax.fori_loop(1, zs, greet_z, 0)
    greet(g, upper)
    greet(g, lower)

    send_load.wait()
    edge_load.wait()
    slot_rows = jnp.broadcast_to(
        send_rows[...][:, None, :], (groups, peer_rows, peer_rows)
    ).reshape(incoming, peer_rows)
    at = lax.broadcasted_iota(jnp.int32, (incoming, peer_rows), 0) % peer_rows
    lane = lax.broadcasted_iota(jnp.int32, (incoming, peer_rows), 1)
    peer_index = jnp.sum(jnp.where(at == lane, slot_rows, 0), axis=1, keepdims=True)
    rim = edge_rows.shape[1]
    at = lax.broadcasted_iota(jnp.int32, (rim, rim), 0)
    lane = lax.broadcasted_iota(jnp.int32, (rim, rim), 1)
    rim_index = [
        jnp.sum(
            jnp.where(at == lane, jnp.broadcast_to(edge_rows[side : side + 1, :], (rim, rim)), 0),
            axis=1,
            keepdims=True,
        )
        for side in (0, 1)
    ]
    pick = one_hot_of(jnp.concatenate([peer_index] + rim_index, axis=0), rows)
    feature_load.wait()
    counts_load = load(counts_hbm, counts, 0)
    cotangent_load = load(cotangent_hbm, cotangent, 1)
    outgoing[0] = dot(pick, features[:, :part]).astype(BF16)
    pl.semaphore_wait(barrier, groups - 1 + xs - 1 + zs - 1 + 2)

    own = pl.ds(pl.multiple_of(g * peer_rows, peer_rows), peer_rows)
    def exchange(c):
        def send_peer(i, carry):
            q = lax.rem(g + i, groups)
            theirs = pl.ds(pl.multiple_of(q * peer_rows, peer_rows), peer_rows)
            pltpu.make_async_remote_copy(
                src_ref=outgoing.at[c, theirs],
                dst_ref=arrived.at[c, own],
                send_sem=a_send.at[c],
                recv_sem=a_recv.at[c],
                device_id={"group": q, "outer": o},
                device_id_type=MESH,
            ).start()
            return carry

        lax.fori_loop(1, groups, send_peer, 0)
        pltpu.make_async_copy(outgoing.at[c, own], arrived.at[c, own], a_recv.at[c]).start()
        for neighbour, start, land in (
            (lower, incoming, incoming + rim),
            (upper, incoming + rim, incoming),
        ):
            pltpu.make_async_remote_copy(
                src_ref=outgoing.at[c, start : start + rim],
                dst_ref=arrived.at[c, land : land + rim],
                send_sem=a_send.at[c],
                recv_sem=a_recv.at[c],
                device_id={"group": g, "outer": neighbour},
                device_id_type=MESH,
            ).start()

    for c in range(chunks):
        if c >= 1:
            outgoing[c] = dot(pick, features[:, c * part : (c + 1) * part]).astype(BF16)
        if c < AHEAD:
            exchange(c)

    own_load = load(self_hbm, own_weight, 2)
    basis_load = load(basis_hbm, basis, 3)

    gain_load.wait()
    source_load.wait()
    counts_load.wait()

    def build(p, carry):
        t, r = lax.div(p, relations), lax.rem(p, relations)
        tiles = [counts[t, r, k].astype(F32) for k in range(slots)]
        row = tile_source[r, pl.ds(t, 1)]
        named = [jnp.broadcast_to(row[:, k : k + 1], (block, block)) for k in range(slots)]
        at_rows = pl.ds(pl.multiple_of(p * block, block), block)
        for s in range(sources):
            held = jnp.zeros((block, block), F32)
            for k in range(slots):
                held = held + jnp.where(named[k] == s, tiles[k], 0.0)
            adjacency[at_rows, s * block : (s + 1) * block] = held.astype(BF16)
        degree = jnp.sum(sum(tiles[1:], tiles[0]), axis=1, keepdims=True)
        inverse = 1.0 / jnp.maximum(degree, 1.0)
        for b in range(2):
            lanes = lax.broadcasted_iota(jnp.int32, (1, relations), 1)
            gain = jnp.sum(
                jnp.where(lanes == r, coefficients[b : b + 1], 0.0), axis=1, keepdims=True
            )
            weight_of[b, at_rows] = jnp.broadcast_to(gain * inverse, (block, block))
        return carry

    lax.fori_loop(0, pairs, build, 0)
    cotangent_load.wait()
    cot_t[...] = jnp.swapaxes(cotangent[...], 0, 1)

    def mix(c):
        cols = slice(c * part, (c + 1) * part)
        pltpu.make_async_copy(arrived.at[c], arrived.at[c], a_recv.at[c]).wait()
        if c + AHEAD < chunks:
            exchange(c + AHEAD)
        for t in range(blocks):
            lo, hi = t * relations * block, (t + 1) * relations * block
            aggregate = dot(adjacency[lo:hi, :rows], features[:, cols]) + dot(
                adjacency[lo:hi, rows:], arrived[c]
            )
            for b in range(2):
                for u in range(part // 128):
                    lanes = slice(u * 128, (u + 1) * 128)
                    value = weight_of[b, lo : lo + block] * aggregate[:block, lanes]
                    for r in range(1, relations):
                        value = value + (
                            weight_of[b, lo + r * block : lo + (r + 1) * block]
                            * aggregate[r * block : (r + 1) * block, lanes]
                        )
                    mixed[b, c, t * block : (t + 1) * block, lanes] = value.astype(BF16)
        core_out[c] = dot(cot_t[...], mixed[1 - core, c]).astype(BF16)
        pltpu.make_async_remote_copy(
            src_ref=core_out.at[c],
            dst_ref=core_in.at[c],
            send_sem=c_send.at[c],
            recv_sem=c_recv.at[c],
            device_id={"group": g + 1 - 2 * core, "outer": o},
            device_id_type=MESH,
        ).start()
        total[c] = dot(cot_t[...], mixed[core, c])

    def along(kind, i):
        if kind == 0:
            there = lax.rem(z + i, zs)
            return there, there * xs + x
        there = lax.rem(x + i, xs)
        return there, z * xs + there

    def spread_first(c):
        pltpu.make_async_copy(core_in.at[c], core_in.at[c], c_recv.at[c]).wait()
        whole = total[c] + core_in[c].astype(F32)
        by_z = whole[:, :half]
        by_x = whole[:, half:]
        by_x = jnp.concatenate(
            [
                by_x[zi * z_rows + xi * tail : zi * z_rows + (xi + 1) * tail]
                for xi in range(xs)
                for zi in range(zs)
            ],
            axis=0,
        )
        for kind, count, value in ((0, zs, by_z), (1, xs, by_x)):
            first_out[c, kind] = value.astype(BF16)
            total[c, :, kind * half : (kind + 1) * half] = value
            size = out_cols // count

            def send(i, carry, kind=kind, size=size, count=count):
                i = lax.rem(3 * i, count)
                there, outer = along(kind, i)
                pltpu.make_async_remote_copy(
                    src_ref=first_out.at[c, kind, pl.ds(pl.multiple_of(there * size, size), size)],
                    dst_ref=first_in.at[c, kind, i - 1],
                    send_sem=f_send.at[c, kind],
                    recv_sem=f_recv.at[c, kind],
                    device_id={"group": g, "outer": outer},
                    device_id_type=MESH,
                ).start()
                return carry

            lax.fori_loop(1, count, send, 0)

    def spread_second(c):
        for kind, count, mine in ((0, zs, z), (1, xs, x)):
            size = out_cols // count
            landed = first_in.at[c, kind]
            pltpu.make_async_copy(landed, landed, f_recv.at[c, kind]).wait()
            held = total[
                c, pl.ds(pl.multiple_of(mine * size, size), size), kind * half : (kind + 1) * half
            ]
            for i in range(count - 1):
                held = held + first_in[c, kind, i].astype(F32)
            second_out[c, kind] = held

            def send(i, carry, kind=kind):
                i = lax.rem(3 * i, (xs, zs)[kind])
                there, outer = along(1 - kind, i)
                pltpu.make_async_remote_copy(
                    src_ref=second_out.at[c, kind, pl.ds(pl.multiple_of(there * tail, tail), tail)],
                    dst_ref=second_in.at[c, kind, i - 1],
                    send_sem=s_send.at[c, kind],
                    recv_sem=s_recv.at[c, kind],
                    device_id={"group": g, "outer": outer},
                    device_id_type=MESH,
                ).start()
                return carry

            lax.fori_loop(1, (xs, zs)[kind], send, 0)

    def spread_third(c):
        for kind, count, mine in ((0, xs, x), (1, zs, z)):
            landed = second_in.at[c, kind]
            pltpu.make_async_copy(landed, landed, s_recv.at[c, kind]).wait()
            held = second_out[c, kind, pl.ds(pl.multiple_of(mine * tail, tail), tail)]
            for i in range(count - 1):
                held = held + second_in[c, kind, i]
            for u in range(half // 128):
                y = (c * part + kind * half) // 128 + u
                third_out[y] = held[:, u * 128 : (u + 1) * 128]
                for q in (2 * y, 2 * y + 1):

                    @pl.when(q != g)
                    def _(y=y, q=q):
                        pltpu.make_async_remote_copy(
                            src_ref=third_out.at[y],
                            dst_ref=third_in.at[g],
                            send_sem=t_send,
                            recv_sem=t_recv,
                            device_id={"group": q, "outer": o},
                            device_id_type=MESH,
                        ).start()

                    @pl.when(q == g)
                    def _(y=y):
                        pltpu.make_async_copy(third_out.at[y], third_in.at[g], t_recv).start()

    for step in range(chunks):
        mix(step)
        spread_first(step)
        if step >= 2:
            spread_second(step - 2)
        if step >= 3:
            spread_third(step - 3)

    own_load.wait()
    basis_load.wait()
    value = dot(features[...], own_weight[...])
    for b in range(2):
        for c in range(chunks):
            value = value + dot(mixed[b, c], basis[b, c * part : (c + 1) * part])
    layer[...] = value.astype(BF16)

    if chunks >= 2:
        spread_second(chunks - 2)
    if chunks >= 3:
        spread_third(chunks - 3)
    spread_second(chunks - 1)
    if chunks >= 2:
        spread_third(chunks - 2)
    spread_third(chunks - 1)

    pltpu.make_async_copy(third_in, third_in, t_recv).wait()
    scale = 1.0 / math.sqrt(rows * groups * zs * xs)
    for b in range(2):
        value = third_in[b]
        for y in range(1, groups // 2):
            value = value + third_in[2 * y + b]
        value = value * scale
        wide = width // groups
        grad_out[b] = jnp.where(core == 0, value[:, :wide], value[:, wide:])

    for c in range(chunks):
        sent = outgoing.at[c, : outgoing.shape[1] - peer_rows]
        pltpu.make_async_copy(sent, sent, a_send.at[c]).wait()
        pltpu.make_async_copy(core_out.at[c], core_out.at[c], c_send.at[c]).wait()
        for kind in (0, 1):
            pltpu.make_async_copy(
                first_in.at[c, kind], first_in.at[c, kind], f_send.at[c, kind]
            ).wait()
            pltpu.make_async_copy(
                second_in.at[c, kind], second_in.at[c, kind], s_send.at[c, kind]
            ).wait()
    sent = third_in.at[: groups - 1]
    pltpu.make_async_copy(sent, sent, t_send).wait()


def hand_over(layer, grad, layer_out, grad_out, sem):
    copies = [
        pltpu.make_async_copy(layer, layer_out, sem.at[0]),
        pltpu.make_async_copy(grad, grad_out, sem.at[1]),
    ]
    for copy in copies:
        copy.start()
    for copy in copies:
        copy.wait()


def shards(
    mesh_sizes,
    features,
    basis_weights,
    self_weight,
    coefficients,
    counts,
    tile_source,
    send_rows,
    edge_rows,
    cotangent,
):
    groups, zs, xs = mesh_sizes
    rows, width = features.shape
    out_cols = cotangent.shape[1]
    blocks, relations, slots, block, _ = counts.shape
    chunks = min(CHUNKS, width // 256)
    part = width // chunks
    half = part // 2
    peers = groups * send_rows.shape[1]
    arriving = peers + 2 * edge_rows.shape[1]
    pairs = blocks * relations
    sizes = (groups, zs, xs, chunks, relations, slots, block)
    z_rows = out_cols // zs
    tail = z_rows // xs
    vmem = pl.BlockSpec(memory_space=pltpu.VMEM)
    anywhere = pl.BlockSpec(memory_space=pl.ANY)
    dma = pltpu.SemaphoreType.DMA
    layer_out, grad = pl.pallas_call(
        functools.partial(layer_kernel, sizes),
        out_shape=(
            pltpu.VMEM((rows, out_cols), BF16),
            pltpu.VMEM((2, tail, width // groups), F32),
        ),
        in_specs=[anywhere] * 9,
        out_specs=(vmem, vmem),
        scratch_shapes=[
            pltpu.VMEM(features.shape, BF16),
            pltpu.VMEM(coefficients.shape[::-1], F32),
            pltpu.VMEM((relations, blocks, slots), jnp.int32),
            pltpu.VMEM(send_rows.shape, jnp.int32),
            pltpu.VMEM(edge_rows.shape, jnp.int32),
            pltpu.VMEM(counts.shape, jnp.int32),
            pltpu.VMEM(basis_weights.shape, BF16),
            pltpu.VMEM(self_weight.shape, BF16),
            pltpu.VMEM((rows, out_cols), BF16),
            pltpu.VMEM((out_cols, rows), BF16),
            pltpu.VMEM((pairs * block, rows + arriving), BF16),
            pltpu.VMEM((2, pairs * block, block), F32),
            pltpu.VMEM((chunks, arriving, part), BF16),
            pltpu.VMEM((chunks, arriving, part), BF16),
            pltpu.VMEM((2, chunks, rows, part), BF16),
            pltpu.VMEM((chunks, out_cols, part), BF16),
            pltpu.VMEM((chunks, out_cols, part), BF16),
            pltpu.VMEM((chunks, out_cols, part), F32),
            pltpu.VMEM((chunks, 2, out_cols, half), BF16),
            pltpu.VMEM((chunks, 2, zs - 1, z_rows, half), BF16),
            pltpu.VMEM((chunks, 2, z_rows, half), F32),
            pltpu.VMEM((chunks, 2, zs - 1, tail, half), F32),
            pltpu.VMEM((groups // 2, tail, 128), F32),
            pltpu.VMEM((groups, tail, 128), F32),
            dma((10,)),
            dma((chunks,)),
            dma((chunks,)),
            dma((chunks,)),
            dma((chunks,)),
            dma((chunks, 2)),
            dma((chunks, 2)),
            dma((chunks, 2)),
            dma((chunks, 2)),
            dma,
            dma,
        ],
        compiler_params=pltpu.CompilerParams(
            collective_id=0, has_side_effects=True, vmem_limit_bytes=56 * 1024 * 1024
        ),
        cost_estimate=pl.CostEstimate(
            flops=3 * 10**9, bytes_accessed=6 * 10**6, transcendentals=0
        ),
        name="graph_layer",
    )(
        features,
        basis_weights,
        self_weight,
        coefficients.T,
        counts,
        tile_source.transpose(1, 0, 2),
        send_rows,
        edge_rows,
        cotangent,
    )
    layer_out, grad = pl.pallas_call(
        hand_over,
        out_shape=(
            jax.ShapeDtypeStruct(layer_out.shape, layer_out.dtype),
            jax.ShapeDtypeStruct(grad.shape, grad.dtype),
        ),
        in_specs=[vmem, vmem],
        out_specs=(anywhere, anywhere),
        scratch_shapes=[dma((2,))],
        compiler_params=pltpu.CompilerParams(vmem_limit_bytes=4 * 1024 * 1024),
        name="hand_over",
    )(layer_out, grad)
    return layer_out, grad.transpose(0, 2, 1)


def solution(mesh):
    groups, outers = mesh.shape["group"], mesh.shape["outer"]
    side = math.isqrt(outers)
    return jax.shard_map(
        functools.partial(shards, (groups, side, side)),
        mesh=mesh,
        in_specs=(
            P(("group", "outer"), None),
            P(),
            P(),
            P(),
            P(("group", "outer"), None, None, None, None),
            P(("group", "outer"), None, None),
            P(("group", "outer"), None),
            P(("group", "outer"), None),
            P(("group", "outer"), None),
        ),
        out_specs=(P(("group", "outer"), None), P(None, "group", "outer")),
        check_vma=False,
    )
```
